32 devices in a mesh: grp: 4 (over y, x), seq: 8 (over z, core).
Axes of the slice: x: 2, y: 2, z: 4, core: 2. Of those that a mesh axis runs over, the one named last changes fastest.
Arguments:
- queries: bfloat16 [4096, 1280], P(('grp', 'seq')), may hold values from -6 to 6
- image_keys: bfloat16 [4096, 1280], P(('grp', 'seq')), may hold values from -6 to 6
- image_values: bfloat16 [4096, 1280], P(('grp', 'seq')), may hold values from -6 to 6
- out_grad: bfloat16 [4096, 1280], P(('grp', 'seq')), may hold values from -6 to 6
- text_keys: bfloat16 [256, 1280], P('seq'), may hold values from -6 to 6
- text_values: bfloat16 [256, 1280], P('seq'), may hold values from -6 to 6
- reward_ranks: int32 [4], replicated, may hold values from 0 to 3, each once
Outputs:
- grad_queries: bfloat16 [4096, 1280], P(('grp', 'seq'))
- grad_keys: bfloat16 [4096, 1280], P(('grp', 'seq'))
- grad_values: bfloat16 [4096, 1280], P(('grp', 'seq'))
- grad_text_keys: bfloat16 [256, 1280], P('seq')
- grad_text_values: bfloat16 [256, 1280], P('seq')
The draws below stay inside these ranges and needn't reach their ends.
Inputs may be any that keep to these rules, and one draw needn't show every extreme that they name: `reward_ranks`: each of the 4 ranks appears once.
All inputs are finite; a program needn't handle non-finite values.
Results may differ from the reference program's by a relative error of at most 0.012.
Values may be sent and summed in bfloat16 or wider, within the bound.
A program may use at most 192 MiB of HBM per device.

```python
import math
import jax
import jax.numpy as jnp
from jax import lax

HEADS = 20
HEAD_DIM = 64
TOK_DEV = 128
TXT = 256
IMG_TOK = 1024
IMAGES = 4
N_SEQ = 8


def draw_queries(key, part):
    key = jax.random.fold_in(key, 3)
    sample = jnp.clip(jax.random.normal(key, (IMAGES * IMG_TOK, HEADS * HEAD_DIM), jnp.float32), -6.0, 6.0)
    return sample.astype(jnp.bfloat16)


def draw_image_keys(key, part):
    key = jax.random.fold_in(key, 4)
    sample = jnp.clip(jax.random.normal(key, (IMAGES * IMG_TOK, HEADS * HEAD_DIM), jnp.float32), -6.0, 6.0)
    return sample.astype(jnp.bfloat16)


def levels(own_key, shape, split, least, high):
    factor_of, own = 1.0, jax.random.fold_in(own_key, 6)
    for position, shards_of in split:
        steps = jnp.exp(jax.random.uniform(jax.random.fold_in(own, position), (shards_of,), jnp.float32, least / len(split), high / len(split)))
        factor_of = factor_of * jnp.repeat(steps, shape[position] // shards_of).reshape([-1 if axis == position else 1 for axis in range(len(shape))])
    return factor_of


def centred(stream_key, dims, width, limit, cuts=(), held_as=jnp.bfloat16):
    factor_of = levels(stream_key, dims, cuts, -0.22, 0.18) if cuts else 1.0
    array = jax.random.normal(stream_key, dims, jnp.float32) * width * factor_of
    return jnp.minimum(jnp.maximum(array, -limit), limit).astype(held_as)


def setup_inputs(seed: int = 0) -> dict:
    splits = jax.random.split(jax.random.key(seed), 8)
    queries = draw_queries(jax.random.fold_in(splits[7], 71), 0)
    image_keys = draw_image_keys(jax.random.fold_in(splits[7], 71), 0)
    image_values = centred(splits[2], (IMAGES * IMG_TOK, HEADS * HEAD_DIM), 1.0, 6.0, ((0, 32),))
    out_grad = centred(splits[3], (IMAGES * IMG_TOK, HEADS * HEAD_DIM), 1.0, 6.0, ((0, 32),))
    text_keys = centred(splits[4], (TXT, HEADS * HEAD_DIM), 1.0, 6.0, ((0, 8),))
    text_values = centred(splits[5], (TXT, HEADS * HEAD_DIM), 1.0, 6.0, ((0, 8),))
    reward_ranks = jax.random.permutation(splits[6], IMAGES).astype(jnp.int32)
    return dict(queries=queries, image_keys=image_keys, image_values=image_values, out_grad=out_grad, text_keys=text_keys, text_values=text_values, reward_ranks=reward_ranks)


def split_heads(matrix):
    return matrix.astype(jnp.float32).reshape(matrix.shape[0], HEADS, HEAD_DIM)

def round_trip(matrix):
    return lax.optimization_barrier(matrix.astype(jnp.bfloat16)).astype(jnp.float32)

def query_block(query_heads, cotan_heads, key_heads, value_heads):
    score_scale = HEAD_DIM ** (-0.5)
    highest = lax.Precision.HIGHEST
    scores = score_scale * jnp.einsum('qhe,khe->hqk', query_heads, key_heads, precision=highest)
    largest = lax.optimization_barrier(jnp.max(scores, -1, keepdims=True))
    log_total = largest + jnp.log(lax.optimization_barrier(jnp.sum(jnp.exp(scores - largest), -1, keepdims=True)))
    probabilities = jnp.exp(scores - log_total)
    products = jnp.einsum('qhe,khe->hqk', cotan_heads, value_heads, precision=highest)
    grad_dot = lax.optimization_barrier(jnp.sum(probabilities * products, -1, keepdims=True))
    weighted = round_trip(probabilities * products)
    probs_low = round_trip(probabilities)
    first_term = jnp.einsum('hqk,khe->hqe', weighted, key_heads, precision=highest)
    second_term = jnp.einsum('hqk,khe->hqe', probs_low, key_heads, precision=highest)
    grad_query = score_scale * (first_term - grad_dot * second_term)
    slopes = round_trip(probabilities * (products - grad_dot))
    key_grads = score_scale * jnp.einsum('hqk,qhe->khe', slopes, query_heads, precision=highest)
    value_grads = jnp.einsum('hqk,qhe->khe', probs_low, cotan_heads, precision=highest)
    return (jnp.transpose(grad_query, (1, 0, 2)), key_grads, value_grads)

def reference(queries, image_keys, image_values, out_grad, text_keys, text_values, reward_ranks):
    features = HEADS * HEAD_DIM
    advantages = (reward_ranks.astype(jnp.float32) - 0.5 * (IMAGES - 1)) / math.sqrt((IMAGES * IMAGES - 1) / 12.0)
    text_key_sum = jnp.zeros((TXT, features), jnp.float32)
    text_value_sum = jnp.zeros((TXT, features), jnp.float32)
    query_parts, key_parts, value_parts = ([], [], [])
    for image_index in range(IMAGES):
        row_start = image_index * IMG_TOK
        query_rows = queries[row_start:row_start + IMG_TOK]
        cotangent = (advantages[image_index] * out_grad[row_start:row_start + IMG_TOK].astype(jnp.float32)).astype(jnp.bfloat16)
        key_heads = split_heads(jnp.concatenate([image_keys[row_start:row_start + IMG_TOK], text_keys], 0))
        value_heads = split_heads(jnp.concatenate([image_values[row_start:row_start + IMG_TOK], text_values], 0))
        query_blocks = split_heads(query_rows).reshape(N_SEQ, TOK_DEV, HEADS, HEAD_DIM)
        cotan_blocks = split_heads(cotangent).reshape(N_SEQ, TOK_DEV, HEADS, HEAD_DIM)

        def advance(running, blocks):
            grad_query, key_grads, value_grads = query_block(blocks[0], blocks[1], key_heads, value_heads)
            return ((running[0] + key_grads, running[1] + value_grads), grad_query)
        empty = jnp.zeros((IMG_TOK + TXT, HEADS, HEAD_DIM), jnp.float32)
        (key_total, value_total), grad_query = lax.scan(advance, (empty, empty), (query_blocks, cotan_blocks))
        query_parts.append(grad_query.reshape(IMG_TOK, features).astype(jnp.bfloat16))
        key_total = key_total.reshape(IMG_TOK + TXT, features)
        value_total = value_total.reshape(IMG_TOK + TXT, features)
        key_parts.append(key_total[:IMG_TOK].astype(jnp.bfloat16))
        value_parts.append(value_total[:IMG_TOK].astype(jnp.bfloat16))
        text_key_sum = text_key_sum + key_total[IMG_TOK:]
        text_value_sum = text_value_sum + value_total[IMG_TOK:]
    return (jnp.concatenate(query_parts, 0), jnp.concatenate(key_parts, 0), jnp.concatenate(value_parts, 0), text_key_sum.astype(jnp.bfloat16), text_value_sum.astype(jnp.bfloat16))
```

```python
import math

import jax
import jax.numpy as jnp
from jax import lax
from jax.experimental import pallas as pl
from jax.experimental.pallas import tpu as pltpu
from jax.sharding import PartitionSpec as P

HEADS = 20
HEAD_DIM = 64


def split_heads(matrix):
    return matrix.reshape(matrix.shape[0], HEADS, HEAD_DIM)


def block_size(rows):
    return math.gcd(rows, 512)


def absorb_block(running, key_rows, value_rows, query_heads, cotan_heads):
    score_scale = HEAD_DIM ** (-0.5)
    highest, summed_weights, weighted_sum = running
    key_heads = split_heads(key_rows)
    value_heads = split_heads(value_rows)
    scores = score_scale * jnp.einsum(
        "qhe,khe->hqk", query_heads, key_heads, preferred_element_type=jnp.float32
    )
    products = jnp.einsum(
        "qhe,khe->hqk", cotan_heads, value_heads, preferred_element_type=jnp.float32
    )
    new_high = jnp.maximum(highest, jnp.max(scores, -1))
    shrink = jnp.exp(highest - new_high)
    weights = jnp.exp(scores - new_high[..., None])
    summed_weights = summed_weights * shrink + jnp.sum(weights, -1)
    weighted_sum = weighted_sum * shrink + jnp.sum(weights * products, -1)
    return (new_high, summed_weights, weighted_sum)


def absorb(running, key_rows, value_rows, query_heads, cotan_heads):
    rows = key_rows.shape[0]
    width = block_size(rows)
    count = rows // width

    def absorb_one(state, pair):
        return (absorb_block(state, pair[0], pair[1], query_heads, cotan_heads), None)

    running, unused = lax.scan(
        absorb_one,
        running,
        (key_rows.reshape(count, width, -1), value_rows.reshape(count, width, -1)),
    )
    return running


def query_block_terms(running, key_rows, value_rows, query_heads, cotan_heads, log_total):
    score_scale = HEAD_DIM ** (-0.5)
    first_sum, second_sum = running
    key_heads = split_heads(key_rows)
    value_heads = split_heads(value_rows)
    scores = score_scale * jnp.einsum(
        "qhe,khe->hqk", query_heads, key_heads, preferred_element_type=jnp.float32
    )
    probabilities = jnp.exp(scores - log_total[..., None])
    products = jnp.einsum(
        "qhe,khe->hqk", cotan_heads, value_heads, preferred_element_type=jnp.float32
    )
    first_sum = first_sum + jnp.einsum(
        "hqk,khe->hqe",
        (probabilities * products).astype(jnp.bfloat16),
        key_heads,
        preferred_element_type=jnp.float32,
    )
    second_sum = second_sum + jnp.einsum(
        "hqk,khe->hqe",
        probabilities.astype(jnp.bfloat16),
        key_heads,
        preferred_element_type=jnp.float32,
    )
    return (first_sum, second_sum)


def query_terms(running, key_rows, value_rows, query_heads, cotan_heads, log_total):
    rows = key_rows.shape[0]
    width = block_size(rows)
    count = rows // width

    def query_one(state, pair):
        return (
            query_block_terms(state, pair[0], pair[1], query_heads, cotan_heads, log_total),
            None,
        )

    running, unused = lax.scan(
        query_one,
        running,
        (key_rows.reshape(count, width, -1), value_rows.reshape(count, width, -1)),
    )
    return running


def key_block_terms(query_heads, cotan_heads, log_total, grad_dot, key_rows, value_rows):
    score_scale = HEAD_DIM ** (-0.5)
    key_heads = split_heads(key_rows)
    value_heads = split_heads(value_rows)
    scores = score_scale * jnp.einsum(
        "qhe,khe->hqk", query_heads, key_heads, preferred_element_type=jnp.float32
    )
    probabilities = jnp.exp(scores - log_total[..., None])
    products = jnp.einsum(
        "qhe,khe->hqk", cotan_heads, value_heads, preferred_element_type=jnp.float32
    )
    slopes = (probabilities * (products - grad_dot[..., None])).astype(jnp.bfloat16)
    key_grads = score_scale * jnp.einsum(
        "hqk,qhe->khe", slopes, query_heads, preferred_element_type=jnp.float32
    )
    value_grads = jnp.einsum(
        "hqk,qhe->khe",
        probabilities.astype(jnp.bfloat16),
        cotan_heads,
        preferred_element_type=jnp.float32,
    )
    return (key_grads.reshape(key_rows.shape[0], -1), value_grads.reshape(key_rows.shape[0], -1))


def key_terms(query_heads, cotan_heads, log_total, grad_dot, key_rows, value_rows):
    rows = query_heads.shape[0]
    width = block_size(rows)
    count = rows // width
    heads_count = log_total.shape[0]
    zero_grads = jnp.zeros((key_rows.shape[0], key_rows.shape[1]), jnp.float32)
    log_blocks = jnp.transpose(log_total.reshape(heads_count, count, width), (1, 0, 2))
    dot_blocks = jnp.transpose(grad_dot.reshape(heads_count, count, width), (1, 0, 2))

    def key_one(state, group):
        key_grads, value_grads = key_block_terms(
            group[0], group[1], group[2], group[3], key_rows, value_rows
        )
        return ((state[0] + key_grads, state[1] + value_grads), None)

    totals, unused = lax.scan(
        key_one,
        (zero_grads, zero_grads),
        (
            query_heads.reshape(count, width, HEADS, HEAD_DIM),
            cotan_heads.reshape(count, width, HEADS, HEAD_DIM),
            log_blocks,
            dot_blocks,
        ),
    )
    return totals


def local(queries, image_keys, image_values, out_grad, text_keys, text_values, reward_ranks):
    row_count = queries.shape[0]
    features = queries.shape[1]
    images_count = reward_ranks.shape[0]
    picked = jnp.sum(
        jnp.where(jnp.arange(images_count) == lax.axis_index("grp"), reward_ranks, 0)
    ).astype(jnp.float32)
    advantage = (picked - 0.5 * (images_count - 1)) / math.sqrt(
        (images_count * images_count - 1) / 12.0
    )
    cotangent = (advantage * out_grad.astype(jnp.float32)).astype(jnp.bfloat16)
    query_heads = split_heads(queries)
    cotan_heads = split_heads(cotangent)
    flat_zero = jnp.zeros((HEADS, row_count), jnp.float32)
    wide_zero = jnp.zeros((HEADS, row_count, HEAD_DIM), jnp.float32)
    start_state = (jnp.full((HEADS, row_count), -1e30, jnp.float32), flat_zero, flat_zero)
    whole_text = (
        lax.all_gather(text_keys, "seq", axis=0, tiled=True),
        lax.all_gather(text_values, "seq", axis=0, tiled=True),
    )
    running = absorb(start_state, whole_text[0], whole_text[1], query_heads, cotan_heads)
    pieces = (
        lax.all_gather(image_keys, "seq", axis=0, tiled=True),
        lax.all_gather(image_values, "seq", axis=0, tiled=True),
    )
    running = absorb(running, pieces[0], pieces[1], query_heads, cotan_heads)
    highest, summed_weights, weighted_sum = running
    log_total = highest + jnp.log(summed_weights)
    grad_dot = weighted_sum / summed_weights
    text_state = query_terms(
        (wide_zero, wide_zero), whole_text[0], whole_text[1], query_heads, cotan_heads, log_total
    )
    pieces = (
        lax.all_gather(image_keys, "seq", axis=0, tiled=True),
        lax.all_gather(image_values, "seq", axis=0, tiled=True),
    )
    first_sum, second_sum = query_terms(
        text_state, pieces[0], pieces[1], query_heads, cotan_heads, log_total
    )
    grad_query = HEAD_DIM ** (-0.5) * (first_sum - grad_dot[..., None] * second_sum)
    grad_queries = (
        jnp.transpose(grad_query, (1, 0, 2)).reshape(row_count, features).astype(jnp.bfloat16)
    )
    all_logs, all_dots = (
        lax.all_gather(log_total.T, "seq", axis=0, tiled=True),
        lax.all_gather(grad_dot.T, "seq", axis=0, tiled=True),
    )
    pieces = (
        lax.all_gather(queries, "seq", axis=0, tiled=True),
        lax.all_gather(cotangent, "seq", axis=0, tiled=True),
    )
    visiting_queries = split_heads(pieces[0])
    visiting_cotans = split_heads(pieces[1])
    key_grads, value_grads = key_terms(
        visiting_queries, visiting_cotans, all_logs.T, all_dots.T, image_keys, image_values
    )
    grad_keys = key_grads.astype(jnp.bfloat16)
    grad_values = value_grads.astype(jnp.bfloat16)
    text_key_part, text_value_part = key_terms(
        query_heads, cotan_heads, log_total, grad_dot, whole_text[0], whole_text[1]
    )
    summed = lax.psum((text_key_part, text_value_part), ("grp", "seq"))
    owned_rows = text_keys.shape[0]
    offset = lax.axis_index("seq") * owned_rows
    text_key_sum = lax.dynamic_slice_in_dim(summed[0], offset, owned_rows, 0)
    text_value_sum = lax.dynamic_slice_in_dim(summed[1], offset, owned_rows, 0)
    return (
        grad_queries,
        grad_keys,
        grad_values,
        text_key_sum.astype(jnp.bfloat16),
        text_value_sum.astype(jnp.bfloat16),
    )


CHIPS = 4
LANES = 128
TILE = 256
MESH = pl.DeviceIdType.MESH
F32 = jnp.float32
BF16 = jnp.bfloat16


def low_lanes(rows):
    return lax.broadcasted_iota(jnp.int32, (rows, LANES), 1) < HEAD_DIM


def swapped(x):
    return pltpu.roll(x.astype(F32), HEAD_DIM, 1)


def pack_head(low, top, bottom):
    mask = low_lanes(top.shape[0])
    if low:
        return jnp.where(mask, top.astype(F32), swapped(bottom))
    return jnp.where(mask, swapped(top), bottom.astype(F32))


def fused(
    ranks, q_in, k_in, v_in, g_in, tk_in, tv_in,
    dq_out, dk_out, dv_out, dtk_out, dtv_out,
    send_a, send_c, recv_a, recv_c, sib_a, sib_c,
    qs, gs, ks, vs, kt, dqs, acc, sib_acc,
    osend_a, osend_c, orecv_a, orecv_c,
    tterm_a, tterm_c, tz_a, tz_c, tzr_a, tzr_c,
    in_s, in_r, sib_s, sib_r, acc_s, acc_r, out_s, out_r, grp_s, grp_r, tz_s, tz_r,
):
    rows = q_in.shape[0]
    text = tk_in.shape[0]
    images = ranks.shape[0]
    grp = lax.axis_index("grp")
    seq = lax.axis_index("seq")
    z = seq // 2
    core = seq % 2

    def peer(step):
        there = (z + step) % CHIPS
        return there, {"seq": there * 2 + core}

    def friend(step):
        there = (grp + step) % images
        return there, {"grp": there}

    sibling = {"seq": z * 2 + 1 - core}

    barrier = pltpu.get_barrier_semaphore()
    for step in range(1, CHIPS):
        pl.semaphore_signal(barrier, inc=1, device_id=peer(step)[1], device_id_type=MESH)
    for step in range(1, images):
        pl.semaphore_signal(barrier, inc=1, device_id=friend(step)[1], device_id_type=MESH)
    pl.semaphore_signal(barrier, inc=1, device_id=sibling, device_id_type=MESH)

    rank = ranks[grp].astype(F32)
    advantage = (jnp.full((1, LANES), rank) - 0.5 * (images - 1)) / math.sqrt(
        (images * images - 1) / 12.0
    )

    def cotangent(columns):
        return (advantage * g_in[:, columns].astype(F32)).astype(BF16)

    def part(t, pair_ref, single_ref):
        return pair_ref.at[t] if t < 2 else single_ref

    sizes = [(rows, text), (rows, text), (rows // 2, text // 2)]

    def pack(t):
        r, n = sizes[t]
        dst = part(t, send_a, send_c)
        for chip in range(CHIPS):
            if t < 2:
                cols = slice((2 * chip + t) * LANES, (2 * chip + t + 1) * LANES)
                pieces = [
                    q_in[:, cols], cotangent(cols), k_in[:, cols], tk_in[:, cols],
                    v_in[:, cols], tv_in[:, cols],
                ]
            else:
                cols = slice((8 + chip // 2) * LANES, (9 + chip // 2) * LANES)
                whole = [
                    q_in[:, cols], cotangent(cols), k_in[:, cols], tk_in[:, cols],
                    v_in[:, cols], tv_in[:, cols],
                ]
                pieces = []
                for x in whole:
                    half = x.shape[0] // 2
                    x = x.astype(F32)
                    pieces.append(pack_head(chip % 2 == 0, x[:half], x[half:]).astype(BF16))
            at = 0
            for x in pieces:
                dst[chip, at : at + x.shape[0], :] = x
                at += x.shape[0]
        part(t, recv_a, recv_c)[z] = dst[z]

    def in_copy(t, step):
        there, device = peer(step)
        return pltpu.make_async_remote_copy(
            src_ref=part(t, send_a, send_c).at[there],
            dst_ref=part(t, recv_a, recv_c).at[z],
            send_sem=in_s.at[t, step],
            recv_sem=in_r.at[t, step],
            device_id=device,
            device_id_type=MESH,
        )

    def sib_copy(t):
        r, n = sizes[t]
        return pltpu.make_async_remote_copy(
            src_ref=part(t, recv_a, recv_c).at[:, pl.ds(2 * r, 2 * r + 2 * n), :],
            dst_ref=part(t, sib_a, sib_c),
            send_sem=sib_s.at[t],
            recv_sem=sib_r.at[t],
            device_id=sibling,
            device_id_type=MESH,
        )

    half_keys = CHIPS * (rows + text)
    queries = CHIPS * rows

    def acc_copy(t):
        return pltpu.make_async_remote_copy(
            src_ref=acc.at[t, :, pl.ds(half_keys, half_keys), :],
            dst_ref=sib_acc.at[t],
            send_sem=acc_s.at[t],
            recv_sem=acc_r.at[t],
            device_id=sibling,
            device_id_type=MESH,
        )

    def out_copy(t, step):
        there, device = peer(step)
        return pltpu.make_async_remote_copy(
            src_ref=part(t, osend_a, osend_c).at[there],
            dst_ref=part(t, orecv_a, orecv_c).at[z],
            send_sem=out_s.at[t, step],
            recv_sem=out_r.at[t, step],
            device_id=device,
            device_id_type=MESH,
        )

    def grp_copy(t, step):
        there, device = friend(step)
        terms = part(t, tterm_a, tterm_c)
        return pltpu.make_async_remote_copy(
            src_ref=terms.at[grp],
            dst_ref=terms.at[grp],
            send_sem=grp_s.at[t, step],
            recv_sem=grp_r.at[t, step],
            device_id=device,
            device_id_type=MESH,
        )

    def tz_copy(t, step):
        there, device = peer(step)
        return pltpu.make_async_remote_copy(
            src_ref=part(t, tz_a, tz_c).at[there],
            dst_ref=part(t, tzr_a, tzr_c).at[z],
            send_sem=tz_s.at[t, step],
            recv_sem=tz_r.at[t, step],
            device_id=device,
            device_id_type=MESH,
        )

    pack(0)
    pl.semaphore_wait(barrier, CHIPS - 1 + images - 1 + 1)
    for t in range(3):
        if t > 0:
            pack(t)
        for step in range(1, CHIPS):
            in_copy(t, step).start()

    factor = HEAD_DIM ** (-0.5) * math.log2(math.e)

    def gathered(x):
        return x.reshape(x.shape[0] * x.shape[1], LANES)

    def unpacked(x):
        return jnp.concatenate([x.astype(F32), swapped(x)], 0).astype(BF16)

    def load_queries(t):
        r, n = sizes[t]
        src = part(t, recv_a, recv_c)
        for dst, at in ((qs, 0), (gs, r)):
            x = gathered(src[:, at : at + r, :])
            mask = low_lanes(queries)
            if t < 2:
                dst[0:queries] = jnp.where(mask, x, jnp.zeros_like(x))
                dst[queries : 2 * queries] = jnp.where(mask, jnp.zeros_like(x), x)
            else:
                x = unpacked(x)
                dst[0:queries] = jnp.where(mask, x, jnp.zeros_like(x))

    def load_keys(t, source, base, at):
        r, n = sizes[t]
        for dst, shift in ((ks, 0), (vs, r + n)):
            x = gathered(source[:, at + shift : at + shift + r + n, :])
            if t == 2:
                x = unpacked(x)
            dst[base : base + half_keys] = x

    def compute(t):
        heads = 2 if t < 2 else 1
        acc[t] = jnp.zeros(acc.shape[1:], F32)
        kt[...] = ks[...].astype(F32).T.astype(BF16)

        def body(i, carry):
            place = pl.ds(pl.multiple_of(i * TILE, TILE), TILE)
            q = qs[place, :]
            g = gs[place, :]
            nt = (((1,), (1,)), ((), ()))
            s = lax.dot_general(ks[...], q, nt, preferred_element_type=F32)
            dp = lax.dot_general(vs[...], g, nt, preferred_element_type=F32)
            e = jnp.exp2((s - jnp.max(s, 0, keepdims=True)) * factor)
            inverse = 1.0 / jnp.sum(e, 0, keepdims=True)
            p = e * inverse
            dot = jnp.sum(p * dp, 0, keepdims=True)
            slopes = (p * (dp - dot)).astype(BF16)
            acc[t, 0] += jnp.dot(slopes, q, preferred_element_type=F32)
            acc[t, 1] += jnp.dot(p.astype(BF16), g, preferred_element_type=F32)
            dqs[place, :] = jnp.dot(kt[...], slopes, preferred_element_type=F32).T
            return carry

        lax.fori_loop(0, heads * queries // TILE, body, 0)

    scale = HEAD_DIM ** (-0.5)

    def finish(t):
        r, n = sizes[t]
        dst = part(t, osend_a, osend_c)
        mask = low_lanes(queries)
        if t < 2:
            x = jnp.where(mask, dqs[0:queries], dqs[queries : 2 * queries])
        else:
            x = pack_head(True, dqs[0 : queries // 2], dqs[queries // 2 : queries])
        dst[:, 0:r, :] = (scale * x).astype(BF16).reshape(CHIPS, r, LANES)
        acc_copy(t).wait_recv()
        terms = part(t, tterm_a, tterm_c)
        for which in range(2):
            x = acc[t, which, 0:half_keys, :] + sib_acc[t, which]
            if which == 0:
                x = scale * x
            if t == 2:
                x = pack_head(True, x[: half_keys // 2], x[half_keys // 2 :])
            x = x.reshape(CHIPS, r + n, LANES)
            dst[:, (1 + which) * r : (2 + which) * r, :] = x[:, :r].astype(BF16)
            terms[grp, :, which * n : (which + 1) * n, :] = x[:, r:]
        for step in range(1, CHIPS):
            out_copy(t, step).start()
        for step in range(1, images):
            grp_copy(t, step).start()
        part(t, orecv_a, orecv_c)[z] = dst[z]

    def finish_text(t):
        terms = part(t, tterm_a, tterm_c)
        for step in range(1, images):
            grp_copy(t, step).wait_recv()
        total = terms[0]
        for image in range(1, images):
            total = total + terms[image]
        dst = part(t, tz_a, tz_c)
        dst[...] = total.astype(BF16)
        for step in range(1, CHIPS):
            tz_copy(t, step).start()
        part(t, tzr_a, tzr_c)[z] = dst[z]

    def place_out(t):
        r, n = sizes[t]
        src = part(t, orecv_a, orecv_c)
        for step in range(1, CHIPS):
            out_copy(t, step).wait_recv()
        for which, dst in ((0, dq_out), (1, dk_out), (2, dv_out)):
            place(t, src, which * r, r, dst)

    def place_text(t):
        r, n = sizes[t]
        src = part(t, tzr_a, tzr_c)
        for step in range(1, CHIPS):
            tz_copy(t, step).wait_recv()
        for which, dst in ((0, dtk_out), (1, dtv_out)):
            place(t, src, which * n, n, dst)

    def place(t, src, at, r, dst):
        if t < 2:
            for chip in range(CHIPS):
                cols = slice((2 * chip + t) * LANES, (2 * chip + t + 1) * LANES)
                dst[:, cols] = src[chip, at : at + r, :]
        else:
            for pair in range(2):
                cols = slice((8 + pair) * LANES, (9 + pair) * LANES)
                low = src[2 * pair, at : at + r, :].astype(F32)
                high = src[2 * pair + 1, at : at + r, :].astype(F32)
                mask = low_lanes(r)
                dst[0:r, cols] = jnp.where(mask, low, swapped(high)).astype(BF16)
                dst[r : 2 * r, cols] = jnp.where(mask, swapped(low), high).astype(BF16)

    for t in range(3):
        r, n = sizes[t]
        for step in range(1, CHIPS):
            in_copy(t, step).wait_recv()
        sib_copy(t).start()
        load_queries(t)
        load_keys(t, part(t, recv_a, recv_c), 0, 2 * r)
        sib_copy(t).wait_recv()
        load_keys(t, part(t, sib_a, sib_c), half_keys, 0)
        compute(t)
        acc_copy(t).start()
        if t > 0:
            finish_text(t - 1)
        finish(t)
    place_out(0)
    place_text(0)
    finish_text(2)
    place_out(1)
    place_text(1)
    place_out(2)
    place_text(2)
    for t in range(3):
        for step in range(1, CHIPS):
            in_copy(t, step).wait_send()
            out_copy(t, step).wait_send()
            tz_copy(t, step).wait_send()
        for step in range(1, images):
            grp_copy(t, step).wait_send()
        sib_copy(t).wait_send()
        acc_copy(t).wait_send()


def exchange(queries, image_keys, image_values, out_grad, text_keys, text_values, reward_ranks):
    rows = queries.shape[0]
    text = text_keys.shape[0]
    images = reward_ranks.shape[0]
    width = 4 * rows + 2 * text
    keys = 2 * CHIPS * (rows + text)
    asked = CHIPS * rows
    like = lambda x: jax.ShapeDtypeStruct(x.shape, BF16)

    def pair_and_single(count, n, dtype):
        return [
            pltpu.VMEM((2, count, n, LANES), dtype),
            pltpu.VMEM((count, n // 2, LANES), dtype),
        ]

    def text_terms(n):
        return [
            pltpu.VMEM((2, images, CHIPS, n, LANES), F32),
            pltpu.VMEM((images, CHIPS, n // 2, LANES), F32),
        ]

    dma = pltpu.SemaphoreType.DMA
    return pl.pallas_call(
        fused,
        out_shape=[like(x) for x in (queries, image_keys, image_values, text_keys, text_values)],
        in_specs=[pl.BlockSpec(memory_space=pltpu.SMEM)]
        + [pl.BlockSpec(memory_space=pltpu.VMEM)] * 6,
        out_specs=[pl.BlockSpec(memory_space=pltpu.VMEM)] * 5,
        scratch_shapes=pair_and_single(CHIPS, width, BF16)
        + pair_and_single(CHIPS, width, BF16)
        + pair_and_single(CHIPS, 2 * rows + 2 * text, BF16)
        + [
            pltpu.VMEM((2 * asked, LANES), BF16),
            pltpu.VMEM((2 * asked, LANES), BF16),
            pltpu.VMEM((keys, LANES), BF16),
            pltpu.VMEM((keys, LANES), BF16),
            pltpu.VMEM((LANES, keys), BF16),
            pltpu.VMEM((2 * asked, LANES), F32),
            pltpu.VMEM((3, 2, keys, LANES), F32),
            pltpu.VMEM((3, 2, keys // 2, LANES), F32),
        ]
        + pair_and_single(CHIPS, 3 * rows, BF16)
        + pair_and_single(CHIPS, 3 * rows, BF16)
        + text_terms(2 * text)
        + pair_and_single(CHIPS, 2 * text, BF16)
        + pair_and_single(CHIPS, 2 * text, BF16)
        + [dma((3, CHIPS)), dma((3, CHIPS)), dma((3,)), dma((3,)), dma((3,)), dma((3,))]
        + [dma((3, CHIPS)), dma((3, CHIPS)), dma((3, images)), dma((3, images))]
        + [dma((3, CHIPS)), dma((3, CHIPS))],
        compiler_params=pltpu.CompilerParams(
            collective_id=0, has_side_effects=True, vmem_limit_bytes=56 * 1024 * 1024
        ),
    )(reward_ranks, queries, image_keys, image_values, out_grad, text_keys, text_values)


def solution(mesh):
    in_specs = (
        P(("grp", "seq"), None),
        P(("grp", "seq"), None),
        P(("grp", "seq"), None),
        P(("grp", "seq"), None),
        P("seq", None),
        P("seq", None),
        P(),
    )
    out_specs = (
        P(("grp", "seq"), None),
        P(("grp", "seq"), None),
        P(("grp", "seq"), None),
        P("seq", None),
        P("seq", None),
    )
    body = exchange if mesh.shape["seq"] == 2 * CHIPS else local
    return jax.shard_map(body, mesh=mesh, in_specs=in_specs, out_specs=out_specs, check_vma=False)
```

```python
import math

import jax
import jax.numpy as jnp
from jax import lax
from jax.experimental import pallas as pl
from jax.experimental.pallas import tpu as pltpu
from jax.sharding import PartitionSpec as P

HEADS = 20
HEAD_DIM = 64


def split_heads(matrix):
    return matrix.reshape(matrix.shape[0], HEADS, HEAD_DIM)


def block_size(rows):
    return math.gcd(rows, 512)


def absorb_block(running, key_rows, value_rows, query_heads, cotan_heads):
    score_scale = HEAD_DIM ** (-0.5)
    highest, summed_weights, weighted_sum = running
    key_heads = split_heads(key_rows)
    value_heads = split_heads(value_rows)
    scores = score_scale * jnp.einsum(
        "qhe,khe->hqk", query_heads, key_heads, preferred_element_type=jnp.float32
    )
    products = jnp.einsum(
        "qhe,khe->hqk", cotan_heads, value_heads, preferred_element_type=jnp.float32
    )
    new_high = jnp.maximum(highest, jnp.max(scores, -1))
    shrink = jnp.exp(highest - new_high)
    weights = jnp.exp(scores - new_high[..., None])
    summed_weights = summed_weights * shrink + jnp.sum(weights, -1)
    weighted_sum = weighted_sum * shrink + jnp.sum(weights * products, -1)
    return (new_high, summed_weights, weighted_sum)


def absorb(running, key_rows, value_rows, query_heads, cotan_heads):
    rows = key_rows.shape[0]
    width = block_size(rows)
    count = rows // width

    def absorb_one(state, pair):
        return (absorb_block(state, pair[0], pair[1], query_heads, cotan_heads), None)

    running, unused = lax.scan(
        absorb_one,
        running,
        (key_rows.reshape(count, width, -1), value_rows.reshape(count, width, -1)),
    )
    return running


def query_block_terms(running, key_rows, value_rows, query_heads, cotan_heads, log_total):
    score_scale = HEAD_DIM ** (-0.5)
    first_sum, second_sum = running
    key_heads = split_heads(key_rows)
    value_heads = split_heads(value_rows)
    scores = score_scale * jnp.einsum(
        "qhe,khe->hqk", query_heads, key_heads, preferred_element_type=jnp.float32
    )
    probabilities = jnp.exp(scores - log_total[..., None])
    products = jnp.einsum(
        "qhe,khe->hqk", cotan_heads, value_heads, preferred_element_type=jnp.float32
    )
    first_sum = first_sum + jnp.einsum(
        "hqk,khe->hqe",
        (probabilities * products).astype(jnp.bfloat16),
        key_heads,
        preferred_element_type=jnp.float32,
    )
    second_sum = second_sum + jnp.einsum(
        "hqk,khe->hqe",
        probabilities.astype(jnp.bfloat16),
        key_heads,
        preferred_element_type=jnp.float32,
    )
    return (first_sum, second_sum)


def query_terms(running, key_rows, value_rows, query_heads, cotan_heads, log_total):
    rows = key_rows.shape[0]
    width = block_size(rows)
    count = rows // width

    def query_one(state, pair):
        return (
            query_block_terms(state, pair[0], pair[1], query_heads, cotan_heads, log_total),
            None,
        )

    running, unused = lax.scan(
        query_one,
        running,
        (key_rows.reshape(count, width, -1), value_rows.reshape(count, width, -1)),
    )
    return running


def key_block_terms(query_heads, cotan_heads, log_total, grad_dot, key_rows, value_rows):
    score_scale = HEAD_DIM ** (-0.5)
    key_heads = split_heads(key_rows)
    value_heads = split_heads(value_rows)
    scores = score_scale * jnp.einsum(
        "qhe,khe->hqk", query_heads, key_heads, preferred_element_type=jnp.float32
    )
    probabilities = jnp.exp(scores - log_total[..., None])
    products = jnp.einsum(
        "qhe,khe->hqk", cotan_heads, value_heads, preferred_element_type=jnp.float32
    )
    slopes = (probabilities * (products - grad_dot[..., None])).astype(jnp.bfloat16)
    key_grads = score_scale * jnp.einsum(
        "hqk,qhe->khe", slopes, query_heads, preferred_element_type=jnp.float32
    )
    value_grads = jnp.einsum(
        "hqk,qhe->khe",
        probabilities.astype(jnp.bfloat16),
        cotan_heads,
        preferred_element_type=jnp.float32,
    )
    return (key_grads.reshape(key_rows.shape[0], -1), value_grads.reshape(key_rows.shape[0], -1))


def key_terms(query_heads, cotan_heads, log_total, grad_dot, key_rows, value_rows):
    rows = query_heads.shape[0]
    width = block_size(rows)
    count = rows // width
    heads_count = log_total.shape[0]
    zero_grads = jnp.zeros((key_rows.shape[0], key_rows.shape[1]), jnp.float32)
    log_blocks = jnp.transpose(log_total.reshape(heads_count, count, width), (1, 0, 2))
    dot_blocks = jnp.transpose(grad_dot.reshape(heads_count, count, width), (1, 0, 2))

    def key_one(state, group):
        key_grads, value_grads = key_block_terms(
            group[0], group[1], group[2], group[3], key_rows, value_rows
        )
        return ((state[0] + key_grads, state[1] + value_grads), None)

    totals, unused = lax.scan(
        key_one,
        (zero_grads, zero_grads),
        (
            query_heads.reshape(count, width, HEADS, HEAD_DIM),
            cotan_heads.reshape(count, width, HEADS, HEAD_DIM),
            log_blocks,
            dot_blocks,
        ),
    )
    return totals


def local(queries, image_keys, image_values, out_grad, text_keys, text_values, reward_ranks):
    row_count = queries.shape[0]
    features = queries.shape[1]
    images_count = reward_ranks.shape[0]
    picked = jnp.sum(
        jnp.where(jnp.arange(images_count) == lax.axis_index("grp"), reward_ranks, 0)
    ).astype(jnp.float32)
    advantage = (picked - 0.5 * (images_count - 1)) / math.sqrt(
        (images_count * images_count - 1) / 12.0
    )
    cotangent = (advantage * out_grad.astype(jnp.float32)).astype(jnp.bfloat16)
    query_heads = split_heads(queries)
    cotan_heads = split_heads(cotangent)
    flat_zero = jnp.zeros((HEADS, row_count), jnp.float32)
    wide_zero = jnp.zeros((HEADS, row_count, HEAD_DIM), jnp.float32)
    start_state = (jnp.full((HEADS, row_count), -1e30, jnp.float32), flat_zero, flat_zero)
    whole_text = (
        lax.all_gather(text_keys, "seq", axis=0, tiled=True),
        lax.all_gather(text_values, "seq", axis=0, tiled=True),
    )
    running = absorb(start_state, whole_text[0], whole_text[1], query_heads, cotan_heads)
    pieces = (
        lax.all_gather(image_keys, "seq", axis=0, tiled=True),
        lax.all_gather(image_values, "seq", axis=0, tiled=True),
    )
    running = absorb(running, pieces[0], pieces[1], query_heads, cotan_heads)
    highest, summed_weights, weighted_sum = running
    log_total = highest + jnp.log(summed_weights)
    grad_dot = weighted_sum / summed_weights
    text_state = query_terms(
        (wide_zero, wide_zero), whole_text[0], whole_text[1], query_heads, cotan_heads, log_total
    )
    pieces = (
        lax.all_gather(image_keys, "seq", axis=0, tiled=True),
        lax.all_gather(image_values, "seq", axis=0, tiled=True),
    )
    first_sum, second_sum = query_terms(
        text_state, pieces[0], pieces[1], query_heads, cotan_heads, log_total
    )
    grad_query = HEAD_DIM ** (-0.5) * (first_sum - grad_dot[..., None] * second_sum)
    grad_queries = (
        jnp.transpose(grad_query, (1, 0, 2)).reshape(row_count, features).astype(jnp.bfloat16)
    )
    all_logs, all_dots = (
        lax.all_gather(log_total.T, "seq", axis=0, tiled=True),
        lax.all_gather(grad_dot.T, "seq", axis=0, tiled=True),
    )
    pieces = (
        lax.all_gather(queries, "seq", axis=0, tiled=True),
        lax.all_gather(cotangent, "seq", axis=0, tiled=True),
    )
    visiting_queries = split_heads(pieces[0])
    visiting_cotans = split_heads(pieces[1])
    key_grads, value_grads = key_terms(
        visiting_queries, visiting_cotans, all_logs.T, all_dots.T, image_keys, image_values
    )
    grad_keys = key_grads.astype(jnp.bfloat16)
    grad_values = value_grads.astype(jnp.bfloat16)
    text_key_part, text_value_part = key_terms(
        query_heads, cotan_heads, log_total, grad_dot, whole_text[0], whole_text[1]
    )
    summed = lax.psum((text_key_part, text_value_part), ("grp", "seq"))
    owned_rows = text_keys.shape[0]
    offset = lax.axis_index("seq") * owned_rows
    text_key_sum = lax.dynamic_slice_in_dim(summed[0], offset, owned_rows, 0)
    text_value_sum = lax.dynamic_slice_in_dim(summed[1], offset, owned_rows, 0)
    return (
        grad_queries,
        grad_keys,
        grad_values,
        text_key_sum.astype(jnp.bfloat16),
        text_value_sum.astype(jnp.bfloat16),
    )


CHIPS = 4
LANES = 128
TILE = 256
MESH = pl.DeviceIdType.MESH
F32 = jnp.float32
BF16 = jnp.bfloat16


def low_lanes(rows):
    return lax.broadcasted_iota(jnp.int32, (rows, LANES), 1) < HEAD_DIM


def swapped(x):
    return pltpu.roll(x.astype(F32), HEAD_DIM, 1)


def pack_head(low, top, bottom):
    mask = low_lanes(top.shape[0])
    if low:
        return jnp.where(mask, top.astype(F32), swapped(bottom))
    return jnp.where(mask, swapped(top), bottom.astype(F32))


def fused(
    ranks, q_in, k_in, v_in, g_in, tk_in, tv_in,
    dq_out, dk_out, dv_out, dtk_out, dtv_out,
    send_a, send_c, recv_a, recv_c, sib_a, sib_c,
    qs, gs, ks, vs, kt, dqs, acc, sib_acc,
    osend_a, osend_c, orecv_a, orecv_c,
    tterm_a, tterm_c, tz_a, tz_c, tzr_a, tzr_c,
    in_s, in_r, sib_s, sib_r, acc_s, acc_r, out_s, out_r, grp_s, grp_r, tz_s, tz_r,
):
    rows = q_in.shape[0]
    text = tk_in.shape[0]
    images = ranks.shape[0]
    grp = lax.axis_index("grp")
    seq = lax.axis_index("seq")
    z = seq // 2
    core = seq % 2

    def peer(step):
        there = (z + step) % CHIPS
        return there, {"seq": there * 2 + core}

    def friend(step):
        there = (grp + step) % images
        return there, {"grp": there}

    sibling = {"seq": z * 2 + 1 - core}

    barrier = pltpu.get_barrier_semaphore()
    for step in range(1, CHIPS):
        pl.semaphore_signal(barrier, inc=1, device_id=peer(step)[1], device_id_type=MESH)
    for step in range(1, images):
        pl.semaphore_signal(barrier, inc=1, device_id=friend(step)[1], device_id_type=MESH)
    pl.semaphore_signal(barrier, inc=1, device_id=sibling, device_id_type=MESH)

    rank = ranks[grp].astype(F32)
    advantage = (jnp.full((1, LANES), rank) - 0.5 * (images - 1)) / math.sqrt(
        (images * images - 1) / 12.0
    )

    def cotangent(columns):
        return (advantage * g_in[:, columns].astype(F32)).astype(BF16)

    def part(t, pair_ref, single_ref):
        return pair_ref.at[t] if t < 2 else single_ref

    sizes = [(rows, text), (rows, text), (rows // 2, text // 2)]

    def pack(t):
        r, n = sizes[t]
        dst = part(t, send_a, send_c)
        for chip in range(CHIPS):
            if t < 2:
                cols = slice((2 * chip + t) * LANES, (2 * chip + t + 1) * LANES)
                pieces = [
                    q_in[:, cols], cotangent(cols), k_in[:, cols], tk_in[:, cols],
                    v_in[:, cols], tv_in[:, cols],
                ]
            else:
                cols = slice((8 + chip // 2) * LANES, (9 + chip // 2) * LANES)
                whole = [
                    q_in[:, cols], cotangent(cols), k_in[:, cols], tk_in[:, cols],
                    v_in[:, cols], tv_in[:, cols],
                ]
                pieces = []
                for x in whole:
                    half = x.shape[0] // 2
                    x = x.astype(F32)
                    pieces.append(pack_head(chip % 2 == 0, x[:half], x[half:]).astype(BF16))
            at = 0
            for x in pieces:
                dst[chip, at : at + x.shape[0], :] = x
                at += x.shape[0]
        part(t, recv_a, recv_c)[z] = dst[z]

    def in_copy(t, step):
        there, device = peer(step)
        return pltpu.make_async_remote_copy(
            src_ref=part(t, send_a, send_c).at[there],
            dst_ref=part(t, recv_a, recv_c).at[z],
            send_sem=in_s.at[t, step],
            recv_sem=in_r.at[t, step],
            device_id=device,
            device_id_type=MESH,
        )

    def sib_copy(t):
        r, n = sizes[t]
        return pltpu.make_async_remote_copy(
            src_ref=part(t, recv_a, recv_c).at[:, pl.ds(2 * r, 2 * r + 2 * n), :],
            dst_ref=part(t, sib_a, sib_c),
            send_sem=sib_s.at[t],
            recv_sem=sib_r.at[t],
            device_id=sibling,
            device_id_type=MESH,
        )

    half_keys = CHIPS * (rows + text)
    queries = CHIPS * rows

    def acc_copy(t):
        return pltpu.make_async_remote_copy(
            src_ref=acc.at[t, :, pl.ds(half_keys, half_keys), :],
            dst_ref=sib_acc.at[t],
            send_sem=acc_s.at[t],
            recv_sem=acc_r.at[t],
            device_id=sibling,
            device_id_type=MESH,
        )

    def out_copy(t, step):
        there, device = peer(step)
        return pltpu.make_async_remote_copy(
            src_ref=part(t, osend_a, osend_c).at[there],
            dst_ref=part(t, orecv_a, orecv_c).at[z],
            send_sem=out_s.at[t, step],
            recv_sem=out_r.at[t, step],
            device_id=device,
            device_id_type=MESH,
        )

    def grp_copy(t, step):
        there, device = friend(step)
        terms = part(t, tterm_a, tterm_c)
        return pltpu.make_async_remote_copy(
            src_ref=terms.at[grp],
            dst_ref=terms.at[grp],
            send_sem=grp_s.at[t, step],
            recv_sem=grp_r.at[t, step],
            device_id=device,
            device_id_type=MESH,
        )

    def tz_copy(t, step):
        there, device = peer(step)
        return pltpu.make_async_remote_copy(
            src_ref=part(t, tz_a, tz_c).at[there],
            dst_ref=part(t, tzr_a, tzr_c).at[z],
            send_sem=tz_s.at[t, step],
            recv_sem=tz_r.at[t, step],
            device_id=device,
            device_id_type=MESH,
        )

    pack(0)
    pl.semaphore_wait(barrier, CHIPS - 1 + images - 1 + 1)
    for t in range(3):
        if t > 0:
            pack(t)
        for step in range(1, CHIPS):
            in_copy(t, step).start()

    factor = HEAD_DIM ** (-0.5) * math.log2(math.e)

    def gathered(x):
        return x.reshape(x.shape[0] * x.shape[1], LANES)

    def unpacked(x):
        return jnp.concatenate([x.astype(F32), swapped(x)], 0).astype(BF16)

    def load_queries(t):
        r, n = sizes[t]
        src = part(t, recv_a, recv_c)
        for dst, at in ((qs, 0), (gs, r)):
            x = gathered(src[:, at : at + r, :])
            mask = low_lanes(queries)
            if t < 2:
                dst[0:queries] = jnp.where(mask, x, jnp.zeros_like(x))
                dst[queries : 2 * queries] = jnp.where(mask, jnp.zeros_like(x), x)
            else:
                x = unpacked(x)
                dst[0:queries] = jnp.where(mask, x, jnp.zeros_like(x))

    def load_keys(t, source, base, at):
        r, n = sizes[t]
        for dst, shift in ((ks, 0), (vs, r + n)):
            x = gathered(source[:, at + shift : at + shift + r + n, :])
            if t == 2:
                x = unpacked(x)
            dst[base : base + half_keys] = x

    def compute(t):
        heads = 2 if t < 2 else 1
        acc[t] = jnp.zeros(acc.shape[1:], F32)
        kt[...] = ks[...].astype(F32).T.astype(BF16)

        def body(i, carry):
            place = pl.ds(pl.multiple_of(i * TILE, TILE), TILE)
            q = qs[place, :]
            g = gs[place, :]
            nt = (((1,), (1,)), ((), ()))
            s = lax.dot_general(ks[...], q, nt, preferred_element_type=F32)
            dp = lax.dot_general(vs[...], g, nt, preferred_element_type=F32)
            e = jnp.exp2((s - jnp.max(s, 0, keepdims=True)) * factor)
            inverse = 1.0 / jnp.sum(e, 0, keepdims=True)
            p = e * inverse
            dot = jnp.sum(p * dp, 0, keepdims=True)
            slopes = (p * (dp - dot)).astype(BF16)
            acc[t, 0] += jnp.dot(slopes, q, preferred_element_type=F32)
            acc[t, 1] += jnp.dot(p.astype(BF16), g, preferred_element_type=F32)
            dqs[place, :] = jnp.dot(kt[...], slopes, preferred_element_type=F32).T
            return carry

        lax.fori_loop(0, heads * queries // TILE, body, 0)

    scale = HEAD_DIM ** (-0.5)

    def finish(t):
        r, n = sizes[t]
        dst = part(t, osend_a, osend_c)
        mask = low_lanes(queries)
        if t < 2:
            x = jnp.where(mask, dqs[0:queries], dqs[queries : 2 * queries])
        else:
            x = pack_head(True, dqs[0 : queries // 2], dqs[queries // 2 : queries])
        dst[:, 0:r, :] = (scale * x).astype(BF16).reshape(CHIPS, r, LANES)
        acc_copy(t).wait_recv()
        terms = part(t, tterm_a, tterm_c)
        for which in range(2):
            x = acc[t, which, 0:half_keys, :] + sib_acc[t, which]
            if which == 0:
                x = scale * x
            if t == 2:
                x = pack_head(True, x[: half_keys // 2], x[half_keys // 2 :])
            x = x.reshape(CHIPS, r + n, LANES)
            dst[:, (1 + which) * r : (2 + which) * r, :] = x[:, :r].astype(BF16)
            terms[grp, :, which * n : (which + 1) * n, :] = x[:, r:]
        for step in range(1, CHIPS):
            out_copy(t, step).start()
        for step in range(1, images):
            grp_copy(t, step).start()
        part(t, orecv_a, orecv_c)[z] = dst[z]

    def finish_text(t):
        terms = part(t, tterm_a, tterm_c)
        for step in range(1, images):
            grp_copy(t, step).wait_recv()
        total = terms[0]
        for image in range(1, images):
            total = total + terms[image]
        dst = part(t, tz_a, tz_c)
        dst[...] = total.astype(BF16)
        for step in range(1, CHIPS):
            tz_copy(t, step).start()
        part(t, tzr_a, tzr_c)[z] = dst[z]

    def place_out(t):
        r, n = sizes[t]
        src = part(t, orecv_a, orecv_c)
        for step in range(1, CHIPS):
            out_copy(t, step).wait_recv()
        for which, dst in ((0, dq_out), (1, dk_out), (2, dv_out)):
            place(t, src, which * r, r, dst)

    def place_text(t):
        r, n = sizes[t]
        src = part(t, tzr_a, tzr_c)
        for step in range(1, CHIPS):
            tz_copy(t, step).wait_recv()
        for which, dst in ((0, dtk_out), (1, dtv_out)):
            place(t, src, which * n, n, dst)

    def place(t, src, at, r, dst):
        if t < 2:
            for chip in range(CHIPS):
                cols = slice((2 * chip + t) * LANES, (2 * chip + t + 1) * LANES)
                dst[:, cols] = src[chip, at : at + r, :]
        else:
            for pair in range(2):
                cols = slice((8 + pair) * LANES, (9 + pair) * LANES)
                low = src[2 * pair, at : at + r, :].astype(F32)
                high = src[2 * pair + 1, at : at + r, :].astype(F32)
                mask = low_lanes(r)
                dst[0:r, cols] = jnp.where(mask, low, swapped(high)).astype(BF16)
                dst[r : 2 * r, cols] = jnp.where(mask, swapped(low), high).astype(BF16)

    for t in range(3):
        r, n = sizes[t]
        for step in range(1, CHIPS):
            in_copy(t, step).wait_recv()
        sib_copy(t).start()
        load_queries(t)
        load_keys(t, part(t, recv_a, recv_c), 0, 2 * r)
        sib_copy(t).wait_recv()
        load_keys(t, part(t, sib_a, sib_c), half_keys, 0)
        compute(t)
        acc_copy(t).start()
        if t > 0:
            finish_text(t - 1)
        finish(t)
    place_out(0)
    place_text(0)
    finish_text(2)
    place_out(1)
    place_text(1)
    place_out(2)
    place_text(2)
    for t in range(3):
        for step in range(1, CHIPS):
            in_copy(t, step).wait_send()
            out_copy(t, step).wait_send()
            tz_copy(t, step).wait_send()
        for step in range(1, images):
            grp_copy(t, step).wait_send()
        sib_copy(t).wait_send()
        acc_copy(t).wait_send()


def write_out(*refs):
    sems = refs[10]
    copies = [pltpu.make_async_copy(refs[i], refs[5 + i], sems.at[i]) for i in range(5)]
    for copy in copies:
        copy.start()
    for copy in copies:
        copy.wait()


def exchange(queries, image_keys, image_values, out_grad, text_keys, text_values, reward_ranks):
    rows = queries.shape[0]
    text = text_keys.shape[0]
    images = reward_ranks.shape[0]
    width = 4 * rows + 2 * text
    keys = 2 * CHIPS * (rows + text)
    asked = CHIPS * rows
    like = lambda x: jax.ShapeDtypeStruct(x.shape, BF16)

    def pair_and_single(count, n, dtype):
        return [
            pltpu.VMEM((2, count, n, LANES), dtype),
            pltpu.VMEM((count, n // 2, LANES), dtype),
        ]

    def text_terms(n):
        return [
            pltpu.VMEM((2, images, CHIPS, n, LANES), F32),
            pltpu.VMEM((images, CHIPS, n // 2, LANES), F32),
        ]

    dma = pltpu.SemaphoreType.DMA
    results = pl.pallas_call(
        fused,
        out_shape=[like(x) for x in (queries, image_keys, image_values, text_keys, text_values)],
        in_specs=[pl.BlockSpec(memory_space=pltpu.SMEM)]
        + [pl.BlockSpec(memory_space=pltpu.VMEM)] * 6,
        out_specs=[pl.BlockSpec(memory_space=pltpu.VMEM)] * 5,
        scratch_shapes=pair_and_single(CHIPS, width, BF16)
        + pair_and_single(CHIPS, width, BF16)
        + pair_and_single(CHIPS, 2 * rows + 2 * text, BF16)
        + [
            pltpu.VMEM((2 * asked, LANES), BF16),
            pltpu.VMEM((2 * asked, LANES), BF16),
            pltpu.VMEM((keys, LANES), BF16),
            pltpu.VMEM((keys, LANES), BF16),
            pltpu.VMEM((LANES, keys), BF16),
            pltpu.VMEM((2 * asked, LANES), F32),
            pltpu.VMEM((3, 2, keys, LANES), F32),
            pltpu.VMEM((3, 2, keys // 2, LANES), F32),
        ]
        + pair_and_single(CHIPS, 3 * rows, BF16)
        + pair_and_single(CHIPS, 3 * rows, BF16)
        + text_terms(2 * text)
        + pair_and_single(CHIPS, 2 * text, BF16)
        + pair_and_single(CHIPS, 2 * text, BF16)
        + [dma((3, CHIPS)), dma((3, CHIPS)), dma((3,)), dma((3,)), dma((3,)), dma((3,))]
        + [dma((3, CHIPS)), dma((3, CHIPS)), dma((3, images)), dma((3, images))]
        + [dma((3, CHIPS)), dma((3, CHIPS))],
        compiler_params=pltpu.CompilerParams(
            collective_id=0, has_side_effects=True, vmem_limit_bytes=56 * 1024 * 1024
        ),
    )(reward_ranks, queries, image_keys, image_values, out_grad, text_keys, text_values)
    return pl.pallas_call(
        write_out,
        out_shape=[like(x) for x in results],
        in_specs=[pl.BlockSpec(memory_space=pltpu.VMEM)] * 5,
        out_specs=[pl.BlockSpec(memory_space=pl.ANY)] * 5,
        scratch_shapes=[dma((5,))],
    )(*results)


def solution(mesh):
    in_specs = (
        P(("grp", "seq"), None),
        P(("grp", "seq"), None),
        P(("grp", "seq"), None),
        P(("grp", "seq"), None),
        P("seq", None),
        P("seq", None),
        P(),
    )
    out_specs = (
        P(("grp", "seq"), None),
        P(("grp", "seq"), None),
        P(("grp", "seq"), None),
        P("seq", None),
        P("seq", None),
    )
    body = exchange if mesh.shape["seq"] == 2 * CHIPS else local
    return jax.shard_map(body, mesh=mesh, in_specs=in_specs, out_specs=out_specs, check_vma=False)
```

```python
import math

import jax
import jax.numpy as jnp
from jax import lax
from jax.experimental import pallas as pl
from jax.experimental.pallas import tpu as pltpu
from jax.sharding import PartitionSpec as P

HEADS = 20
HEAD_DIM = 64


def split_heads(matrix):
    return matrix.reshape(matrix.shape[0], HEADS, HEAD_DIM)


def block_size(rows):
    return math.gcd(rows, 512)


def absorb_block(running, key_rows, value_rows, query_heads, cotan_heads):
    score_scale = HEAD_DIM ** (-0.5)
    highest, summed_weights, weighted_sum = running
    key_heads = split_heads(key_rows)
    value_heads = split_heads(value_rows)
    scores = score_scale * jnp.einsum(
        "qhe,khe->hqk", query_heads, key_heads, preferred_element_type=jnp.float32
    )
    products = jnp.einsum(
        "qhe,khe->hqk", cotan_heads, value_heads, preferred_element_type=jnp.float32
    )
    new_high = jnp.maximum(highest, jnp.max(scores, -1))
    shrink = jnp.exp(highest - new_high)
    weights = jnp.exp(scores - new_high[..., None])
    summed_weights = summed_weights * shrink + jnp.sum(weights, -1)
    weighted_sum = weighted_sum * shrink + jnp.sum(weights * products, -1)
    return (new_high, summed_weights, weighted_sum)


def absorb(running, key_rows, value_rows, query_heads, cotan_heads):
    rows = key_rows.shape[0]
    width = block_size(rows)
    count = rows // width

    def absorb_one(state, pair):
        return (absorb_block(state, pair[0], pair[1], query_heads, cotan_heads), None)

    running, unused = lax.scan(
        absorb_one,
        running,
        (key_rows.reshape(count, width, -1), value_rows.reshape(count, width, -1)),
    )
    return running


def query_block_terms(running, key_rows, value_rows, query_heads, cotan_heads, log_total):
    score_scale = HEAD_DIM ** (-0.5)
    first_sum, second_sum = running
    key_heads = split_heads(key_rows)
    value_heads = split_heads(value_rows)
    scores = score_scale * jnp.einsum(
        "qhe,khe->hqk", query_heads, key_heads, preferred_element_type=jnp.float32
    )
    probabilities = jnp.exp(scores - log_total[..., None])
    products = jnp.einsum(
        "qhe,khe->hqk", cotan_heads, value_heads, preferred_element_type=jnp.float32
    )
    first_sum = first_sum + jnp.einsum(
        "hqk,khe->hqe",
        (probabilities * products).astype(jnp.bfloat16),
        key_heads,
        preferred_element_type=jnp.float32,
    )
    second_sum = second_sum + jnp.einsum(
        "hqk,khe->hqe",
        probabilities.astype(jnp.bfloat16),
        key_heads,
        preferred_element_type=jnp.float32,
    )
    return (first_sum, second_sum)


def query_terms(running, key_rows, value_rows, query_heads, cotan_heads, log_total):
    rows = key_rows.shape[0]
    width = block_size(rows)
    count = rows // width

    def query_one(state, pair):
        return (
            query_block_terms(state, pair[0], pair[1], query_heads, cotan_heads, log_total),
            None,
        )

    running, unused = lax.scan(
        query_one,
        running,
        (key_rows.reshape(count, width, -1), value_rows.reshape(count, width, -1)),
    )
    return running


def key_block_terms(query_heads, cotan_heads, log_total, grad_dot, key_rows, value_rows):
    score_scale = HEAD_DIM ** (-0.5)
    key_heads = split_heads(key_rows)
    value_heads = split_heads(value_rows)
    scores = score_scale * jnp.einsum(
        "qhe,khe->hqk", query_heads, key_heads, preferred_element_type=jnp.float32
    )
    probabilities = jnp.exp(scores - log_total[..., None])
    products = jnp.einsum(
        "qhe,khe->hqk", cotan_heads, value_heads, preferred_element_type=jnp.float32
    )
    slopes = (probabilities * (products - grad_dot[..., None])).astype(jnp.bfloat16)
    key_grads = score_scale * jnp.einsum(
        "hqk,qhe->khe", slopes, query_heads, preferred_element_type=jnp.float32
    )
    value_grads = jnp.einsum(
        "hqk,qhe->khe",
        probabilities.astype(jnp.bfloat16),
        cotan_heads,
        preferred_element_type=jnp.float32,
    )
    return (key_grads.reshape(key_rows.shape[0], -1), value_grads.reshape(key_rows.shape[0], -1))


def key_terms(query_heads, cotan_heads, log_total, grad_dot, key_rows, value_rows):
    rows = query_heads.shape[0]
    width = block_size(rows)
    count = rows // width
    heads_count = log_total.shape[0]
    zero_grads = jnp.zeros((key_rows.shape[0], key_rows.shape[1]), jnp.float32)
    log_blocks = jnp.transpose(log_total.reshape(heads_count, count, width), (1, 0, 2))
    dot_blocks = jnp.transpose(grad_dot.reshape(heads_count, count, width), (1, 0, 2))

    def key_one(state, group):
        key_grads, value_grads = key_block_terms(
            group[0], group[1], group[2], group[3], key_rows, value_rows
        )
        return ((state[0] + key_grads, state[1] + value_grads), None)

    totals, unused = lax.scan(
        key_one,
        (zero_grads, zero_grads),
        (
            query_heads.reshape(count, width, HEADS, HEAD_DIM),
            cotan_heads.reshape(count, width, HEADS, HEAD_DIM),
            log_blocks,
            dot_blocks,
        ),
    )
    return totals


def local(queries, image_keys, image_values, out_grad, text_keys, text_values, reward_ranks):
    row_count = queries.shape[0]
    features = queries.shape[1]
    images_count = reward_ranks.shape[0]
    picked = jnp.sum(
        jnp.where(jnp.arange(images_count) == lax.axis_index("grp"), reward_ranks, 0)
    ).astype(jnp.float32)
    advantage = (picked - 0.5 * (images_count - 1)) / math.sqrt(
        (images_count * images_count - 1) / 12.0
    )
    cotangent = (advantage * out_grad.astype(jnp.float32)).astype(jnp.bfloat16)
    query_heads = split_heads(queries)
    cotan_heads = split_heads(cotangent)
    flat_zero = jnp.zeros((HEADS, row_count), jnp.float32)
    wide_zero = jnp.zeros((HEADS, row_count, HEAD_DIM), jnp.float32)
    start_state = (jnp.full((HEADS, row_count), -1e30, jnp.float32), flat_zero, flat_zero)
    whole_text = (
        lax.all_gather(text_keys, "seq", axis=0, tiled=True),
        lax.all_gather(text_values, "seq", axis=0, tiled=True),
    )
    running = absorb(start_state, whole_text[0], whole_text[1], query_heads, cotan_heads)
    pieces = (
        lax.all_gather(image_keys, "seq", axis=0, tiled=True),
        lax.all_gather(image_values, "seq", axis=0, tiled=True),
    )
    running = absorb(running, pieces[0], pieces[1], query_heads, cotan_heads)
    highest, summed_weights, weighted_sum = running
    log_total = highest + jnp.log(summed_weights)
    grad_dot = weighted_sum / summed_weights
    text_state = query_terms(
        (wide_zero, wide_zero), whole_text[0], whole_text[1], query_heads, cotan_heads, log_total
    )
    pieces = (
        lax.all_gather(image_keys, "seq", axis=0, tiled=True),
        lax.all_gather(image_values, "seq", axis=0, tiled=True),
    )
    first_sum, second_sum = query_terms(
        text_state, pieces[0], pieces[1], query_heads, cotan_heads, log_total
    )
    grad_query = HEAD_DIM ** (-0.5) * (first_sum - grad_dot[..., None] * second_sum)
    grad_queries = (
        jnp.transpose(grad_query, (1, 0, 2)).reshape(row_count, features).astype(jnp.bfloat16)
    )
    all_logs, all_dots = (
        lax.all_gather(log_total.T, "seq", axis=0, tiled=True),
        lax.all_gather(grad_dot.T, "seq", axis=0, tiled=True),
    )
    pieces = (
        lax.all_gather(queries, "seq", axis=0, tiled=True),
        lax.all_gather(cotangent, "seq", axis=0, tiled=True),
    )
    visiting_queries = split_heads(pieces[0])
    visiting_cotans = split_heads(pieces[1])
    key_grads, value_grads = key_terms(
        visiting_queries, visiting_cotans, all_logs.T, all_dots.T, image_keys, image_values
    )
    grad_keys = key_grads.astype(jnp.bfloat16)
    grad_values = value_grads.astype(jnp.bfloat16)
    text_key_part, text_value_part = key_terms(
        query_heads, cotan_heads, log_total, grad_dot, whole_text[0], whole_text[1]
    )
    summed = lax.psum((text_key_part, text_value_part), ("grp", "seq"))
    owned_rows = text_keys.shape[0]
    offset = lax.axis_index("seq") * owned_rows
    text_key_sum = lax.dynamic_slice_in_dim(summed[0], offset, owned_rows, 0)
    text_value_sum = lax.dynamic_slice_in_dim(summed[1], offset, owned_rows, 0)
    return (
        grad_queries,
        grad_keys,
        grad_values,
        text_key_sum.astype(jnp.bfloat16),
        text_value_sum.astype(jnp.bfloat16),
    )


CHIPS = 4
LANES = 128
TILE = 256
MESH = pl.DeviceIdType.MESH
F32 = jnp.float32
BF16 = jnp.bfloat16


def low_lanes(rows):
    return lax.broadcasted_iota(jnp.int32, (rows, LANES), 1) < HEAD_DIM


def swapped(x):
    return pltpu.roll(x.astype(F32), HEAD_DIM, 1)


def pack_head(low, top, bottom):
    mask = low_lanes(top.shape[0])
    if low:
        return jnp.where(mask, top.astype(F32), swapped(bottom))
    return jnp.where(mask, swapped(top), bottom.astype(F32))


def fused(
    ranks, q_in, k_in, v_in, g_in, tk_in, tv_in,
    dq_out, dk_out, dv_out, dtk_out, dtv_out,
    send_a, send_c, recv_a, recv_c, sib_a, sib_c,
    qs, gs, ks, vs, kt, dqs, acc, sib_acc,
    osend_a, osend_c, orecv_a, orecv_c,
    tsend, tterm_a, tterm_c, tz_a, tz_c, tshare, tzr_c,
    in_s, in_r, sib_s, sib_r, acc_s, acc_r, out_s, out_r, grp_s, grp_r, tz_s, tz_r, share_s, share_r,
):
    rows = q_in.shape[0]
    text = tk_in.shape[0]
    images = ranks.shape[0]
    grp = lax.axis_index("grp")
    seq = lax.axis_index("seq")
    z = seq // 2
    core = seq % 2

    def peer(step):
        there = (z + step) % CHIPS
        return there, {"seq": there * 2 + core}

    def friend(step):
        there = (grp + step) % images
        return there, {"grp": there}

    sibling = {"seq": z * 2 + 1 - core}

    barrier = pltpu.get_barrier_semaphore()
    for step in range(1, CHIPS):
        pl.semaphore_signal(barrier, inc=1, device_id=peer(step)[1], device_id_type=MESH)
    for step in range(1, images):
        pl.semaphore_signal(barrier, inc=1, device_id=friend(step)[1], device_id_type=MESH)
    pl.semaphore_signal(barrier, inc=1, device_id=sibling, device_id_type=MESH)

    rank = ranks[grp].astype(F32)
    advantage = (jnp.full((1, LANES), rank) - 0.5 * (images - 1)) / math.sqrt(
        (images * images - 1) / 12.0
    )

    def cotangent(columns):
        return (advantage * g_in[:, columns].astype(F32)).astype(BF16)

    def part(t, pair_ref, single_ref):
        return pair_ref.at[t] if t < 2 else single_ref

    sizes = [(rows, text), (rows, text), (rows // 2, text // 2)]

    def pack(t):
        r, n = sizes[t]
        dst = part(t, send_a, send_c)
        for chip in range(CHIPS):
            if t < 2:
                cols = slice((2 * chip + t) * LANES, (2 * chip + t + 1) * LANES)
                pieces = [
                    q_in[:, cols], cotangent(cols), k_in[:, cols], tk_in[:, cols],
                    v_in[:, cols], tv_in[:, cols],
                ]
            else:
                cols = slice((8 + chip // 2) * LANES, (9 + chip // 2) * LANES)
                whole = [
                    q_in[:, cols], cotangent(cols), k_in[:, cols], tk_in[:, cols],
                    v_in[:, cols], tv_in[:, cols],
                ]
                pieces = []
                for x in whole:
                    half = x.shape[0] // 2
                    x = x.astype(F32)
                    pieces.append(pack_head(chip % 2 == 0, x[:half], x[half:]).astype(BF16))
            at = 0
            for x in pieces:
                dst[chip, at : at + x.shape[0], :] = x
                at += x.shape[0]
        part(t, recv_a, recv_c)[z] = dst[z]

    def in_copy(t, step):
        there, device = peer(step)
        return pltpu.make_async_remote_copy(
            src_ref=part(t, send_a, send_c).at[there],
            dst_ref=part(t, recv_a, recv_c).at[z],
            send_sem=in_s.at[t, step],
            recv_sem=in_r.at[t, step],
            device_id=device,
            device_id_type=MESH,
        )

    def sib_copy(t):
        r, n = sizes[t]
        return pltpu.make_async_remote_copy(
            src_ref=part(t, recv_a, recv_c).at[:, pl.ds(2 * r, 2 * r + 2 * n), :],
            dst_ref=part(t, sib_a, sib_c),
            send_sem=sib_s.at[t],
            recv_sem=sib_r.at[t],
            device_id=sibling,
            device_id_type=MESH,
        )

    half_keys = CHIPS * (rows + text)
    queries = CHIPS * rows

    def acc_copy(t):
        return pltpu.make_async_remote_copy(
            src_ref=acc.at[t, :, pl.ds(half_keys, half_keys), :],
            dst_ref=sib_acc.at[t],
            send_sem=acc_s.at[t],
            recv_sem=acc_r.at[t],
            device_id=sibling,
            device_id_type=MESH,
        )

    def out_copy(t, step):
        there, device = peer(step)
        return pltpu.make_async_remote_copy(
            src_ref=part(t, osend_a, osend_c).at[there],
            dst_ref=part(t, orecv_a, orecv_c).at[z],
            send_sem=out_s.at[t, step],
            recv_sem=out_r.at[t, step],
            device_id=device,
            device_id_type=MESH,
        )

    share = 2 * text // images

    def grp_copy(t, step):
        there, device = friend(step)
        if t < 2:
            src = tsend.at[t, there]
            dst = tterm_a.at[t, grp]
        else:
            src = tterm_c.at[grp]
            dst = tterm_c.at[grp]
        return pltpu.make_async_remote_copy(
            src_ref=src,
            dst_ref=dst,
            send_sem=grp_s.at[t, step],
            recv_sem=grp_r.at[t, step],
            device_id=device,
            device_id_type=MESH,
        )

    def share_copy(t, step):
        there, device = friend(step)
        return pltpu.make_async_remote_copy(
            src_ref=tshare.at[t, grp],
            dst_ref=tshare.at[t, grp],
            send_sem=share_s.at[t, step],
            recv_sem=share_r.at[t, step],
            device_id=device,
            device_id_type=MESH,
        )

    def tz_copy(t, step):
        there, device = peer(step)
        return pltpu.make_async_remote_copy(
            src_ref=(tz_a.at[t] if t < 2 else tz_c).at[there],
            dst_ref=tshare.at[t, grp, z] if t < 2 else tzr_c.at[z],
            send_sem=tz_s.at[t, step],
            recv_sem=tz_r.at[t, step],
            device_id=device,
            device_id_type=MESH,
        )

    pack(0)
    pl.semaphore_wait(barrier, CHIPS - 1 + images - 1 + 1)
    for t in range(3):
        if t > 0:
            pack(t)
        for step in range(1, CHIPS):
            in_copy(t, step).start()

    factor = HEAD_DIM ** (-0.5) * math.log2(math.e)

    def gathered(x):
        return x.reshape(x.shape[0] * x.shape[1], LANES)

    def unpacked(x):
        return jnp.concatenate([x.astype(F32), swapped(x)], 0).astype(BF16)

    def load_queries(t):
        r, n = sizes[t]
        src = part(t, recv_a, recv_c)
        for dst, at in ((qs, 0), (gs, r)):
            x = gathered(src[:, at : at + r, :])
            mask = low_lanes(queries)
            if t < 2:
                dst[0:queries] = jnp.where(mask, x, jnp.zeros_like(x))
                dst[queries : 2 * queries] = jnp.where(mask, jnp.zeros_like(x), x)
            else:
                x = unpacked(x)
                dst[0:queries] = jnp.where(mask, x, jnp.zeros_like(x))

    def load_keys(t, source, base, at):
        r, n = sizes[t]
        for dst, shift in ((ks, 0), (vs, r + n)):
            x = gathered(source[:, at + shift : at + shift + r + n, :])
            if t == 2:
                x = unpacked(x)
            dst[base : base + half_keys] = x

    def compute(t):
        heads = 2 if t < 2 else 1
        acc[t] = jnp.zeros(acc.shape[1:], F32)
        kt[...] = ks[...].astype(F32).T.astype(BF16)

        def body(i, carry):
            place = pl.ds(pl.multiple_of(i * TILE, TILE), TILE)
            q = qs[place, :]
            g = gs[place, :]
            nt = (((1,), (1,)), ((), ()))
            s = lax.dot_general(ks[...], q, nt, preferred_element_type=F32)
            dp = lax.dot_general(vs[...], g, nt, preferred_element_type=F32)
            e = jnp.exp2((s - jnp.max(s, 0, keepdims=True)) * factor)
            inverse = 1.0 / jnp.sum(e, 0, keepdims=True)
            p = e * inverse
            dot = jnp.sum(p * dp, 0, keepdims=True)
            slopes = (p * (dp - dot)).astype(BF16)
            acc[t, 0] += jnp.dot(slopes, q, preferred_element_type=F32)
            acc[t, 1] += jnp.dot(p.astype(BF16), g, preferred_element_type=F32)
            dqs[place, :] = jnp.dot(kt[...], slopes, preferred_element_type=F32).T
            return carry

        lax.fori_loop(0, heads * queries // TILE, body, 0)

    scale = HEAD_DIM ** (-0.5)

    def finish(t):
        r, n = sizes[t]
        dst = part(t, osend_a, osend_c)
        mask = low_lanes(queries)
        if t < 2:
            x = jnp.where(mask, dqs[0:queries], dqs[queries : 2 * queries])
        else:
            x = pack_head(True, dqs[0 : queries // 2], dqs[queries // 2 : queries])
        dst[:, 0:r, :] = (scale * x).astype(BF16).reshape(CHIPS, r, LANES)
        acc_copy(t).wait_recv()
        for which in range(2):
            x = acc[t, which, 0:half_keys, :] + sib_acc[t, which]
            if which == 0:
                x = scale * x
            if t == 2:
                x = pack_head(True, x[: half_keys // 2], x[half_keys // 2 :])
            x = x.reshape(CHIPS, r + n, LANES)
            dst[:, (1 + which) * r : (2 + which) * r, :] = x[:, :r].astype(BF16)
            if t < 2:
                half = images // 2
                for j in range(half):
                    tsend[t, which * half + j] = x[:, r + j * share : r + (j + 1) * share]
            else:
                tterm_c[grp, :, which * n : (which + 1) * n, :] = x[:, r:]
        for step in range(1, CHIPS):
            out_copy(t, step).start()
        for step in range(1, images):
            grp_copy(t, step).start()
        if t < 2:
            tterm_a[t, grp] = tsend[t, grp]
        part(t, orecv_a, orecv_c)[z] = dst[z]

    def finish_text(t):
        terms = part(t, tterm_a, tterm_c)
        for step in range(1, images):
            grp_copy(t, step).wait_recv()
        total = terms[0]
        for image in range(1, images):
            total = total + terms[image]
        dst = part(t, tz_a, tz_c)
        dst[...] = total.astype(BF16)
        for step in range(1, CHIPS):
            tz_copy(t, step).start()
        if t < 2:
            tshare[t, grp, z] = dst[z]
        else:
            tzr_c[z] = dst[z]

    def share_text(t):
        for step in range(1, CHIPS):
            tz_copy(t, step).wait_recv()
        for step in range(1, images):
            share_copy(t, step).start()

    def place_out(t):
        r, n = sizes[t]
        src = part(t, orecv_a, orecv_c)
        for step in range(1, CHIPS):
            out_copy(t, step).wait_recv()
        for which, dst in ((0, dq_out), (1, dk_out), (2, dv_out)):
            place(t, src, which * r, r, dst)

    def place_text(t):
        r, n = sizes[t]
        if t < 2:
            for step in range(1, images):
                share_copy(t, step).wait_recv()
            half = images // 2
            for which, dst in ((0, dtk_out), (1, dtv_out)):
                for chip in range(CHIPS):
                    cols = slice((2 * chip + t) * LANES, (2 * chip + t + 1) * LANES)
                    for j in range(half):
                        dst[j * share : (j + 1) * share, cols] = tshare[t, which * half + j, chip]
            return
        for step in range(1, CHIPS):
            tz_copy(t, step).wait_recv()
        for which, dst in ((0, dtk_out), (1, dtv_out)):
            place(t, tzr_c, which * n, n, dst)

    def place(t, src, at, r, dst):
        if t < 2:
            for chip in range(CHIPS):
                cols = slice((2 * chip + t) * LANES, (2 * chip + t + 1) * LANES)
                dst[:, cols] = src[chip, at : at + r, :]
        else:
            for pair in range(2):
                cols = slice((8 + pair) * LANES, (9 + pair) * LANES)
                low = src[2 * pair, at : at + r, :].astype(F32)
                high = src[2 * pair + 1, at : at + r, :].astype(F32)
                mask = low_lanes(r)
                dst[0:r, cols] = jnp.where(mask, low, swapped(high)).astype(BF16)
                dst[r : 2 * r, cols] = jnp.where(mask, swapped(low), high).astype(BF16)

    for t in range(3):
        r, n = sizes[t]
        for step in range(1, CHIPS):
            in_copy(t, step).wait_recv()
        sib_copy(t).start()
        load_queries(t)
        load_keys(t, part(t, recv_a, recv_c), 0, 2 * r)
        sib_copy(t).wait_recv()
        load_keys(t, part(t, sib_a, sib_c), half_keys, 0)
        compute(t)
        acc_copy(t).start()
        if t > 0:
            finish_text(t - 1)
        finish(t)
    share_text(0)
    finish_text(2)
    share_text(1)
    place_out(0)
    place_text(0)
    place_out(1)
    place_text(1)
    place_out(2)
    place_text(2)
    for t in range(3):
        for step in range(1, CHIPS):
            in_copy(t, step).wait_send()
            out_copy(t, step).wait_send()
            tz_copy(t, step).wait_send()
        for step in range(1, images):
            grp_copy(t, step).wait_send()
            if t < 2:
                share_copy(t, step).wait_send()
        sib_copy(t).wait_send()
        acc_copy(t).wait_send()


def write_out(*refs):
    sems = refs[10]
    copies = [pltpu.make_async_copy(refs[i], refs[5 + i], sems.at[i]) for i in range(5)]
    for copy in copies:
        copy.start()
    for copy in copies:
        copy.wait()


def exchange(queries, image_keys, image_values, out_grad, text_keys, text_values, reward_ranks):
    rows = queries.shape[0]
    text = text_keys.shape[0]
    images = reward_ranks.shape[0]
    width = 4 * rows + 2 * text
    keys = 2 * CHIPS * (rows + text)
    asked = CHIPS * rows
    like = lambda x: jax.ShapeDtypeStruct(x.shape, BF16)

    def pair_and_single(count, n, dtype):
        return [
            pltpu.VMEM((2, count, n, LANES), dtype),
            pltpu.VMEM((count, n // 2, LANES), dtype),
        ]

    def text_terms(n):
        return [
            pltpu.VMEM((2, images, CHIPS, n // images, LANES), F32),
            pltpu.VMEM((2, images, CHIPS, n // images, LANES), F32),
            pltpu.VMEM((images, CHIPS, n // 2, LANES), F32),
        ]

    dma = pltpu.SemaphoreType.DMA
    results = pl.pallas_call(
        fused,
        out_shape=[like(x) for x in (queries, image_keys, image_values, text_keys, text_values)],
        in_specs=[pl.BlockSpec(memory_space=pltpu.SMEM)]
        + [pl.BlockSpec(memory_space=pltpu.VMEM)] * 6,
        out_specs=[pl.BlockSpec(memory_space=pltpu.VMEM)] * 5,
        scratch_shapes=pair_and_single(CHIPS, width, BF16)
        + pair_and_single(CHIPS, width, BF16)
        + pair_and_single(CHIPS, 2 * rows + 2 * text, BF16)
        + [
            pltpu.VMEM((2 * asked, LANES), BF16),
            pltpu.VMEM((2 * asked, LANES), BF16),
            pltpu.VMEM((keys, LANES), BF16),
            pltpu.VMEM((keys, LANES), BF16),
            pltpu.VMEM((LANES, keys), BF16),
            pltpu.VMEM((2 * asked, LANES), F32),
            pltpu.VMEM((3, 2, keys, LANES), F32),
            pltpu.VMEM((3, 2, keys // 2, LANES), F32),
        ]
        + pair_and_single(CHIPS, 3 * rows, BF16)
        + pair_and_single(CHIPS, 3 * rows, BF16)
        + text_terms(2 * text)
        + [
            pltpu.VMEM((2, CHIPS, 2 * text // images, LANES), BF16),
            pltpu.VMEM((CHIPS, text, LANES), BF16),
            pltpu.VMEM((2, images, CHIPS, 2 * text // images, LANES), BF16),
            pltpu.VMEM((CHIPS, text, LANES), BF16),
        ]
        + [dma((3, CHIPS)), dma((3, CHIPS)), dma((3,)), dma((3,)), dma((3,)), dma((3,))]
        + [dma((3, CHIPS)), dma((3, CHIPS)), dma((3, images)), dma((3, images))]
        + [dma((3, CHIPS)), dma((3, CHIPS)), dma((2, images)), dma((2, images))],
        compiler_params=pltpu.CompilerParams(
            collective_id=0, has_side_effects=True, vmem_limit_bytes=56 * 1024 * 1024
        ),
    )(reward_ranks, queries, image_keys, image_values, out_grad, text_keys, text_values)
    return pl.pallas_call(
        write_out,
        out_shape=[like(x) for x in results],
        in_specs=[pl.BlockSpec(memory_space=pltpu.VMEM)] * 5,
        out_specs=[pl.BlockSpec(memory_space=pl.ANY)] * 5,
        scratch_shapes=[dma((5,))],
    )(*results)


def solution(mesh):
    in_specs = (
        P(("grp", "seq"), None),
        P(("grp", "seq"), None),
        P(("grp", "seq"), None),
        P(("grp", "seq"), None),
        P("seq", None),
        P("seq", None),
        P(),
    )
    out_specs = (
        P(("grp", "seq"), None),
        P(("grp", "seq"), None),
        P(("grp", "seq"), None),
        P("seq", None),
        P("seq", None),
    )
    body = exchange if mesh.shape["seq"] == 2 * CHIPS else local
    return jax.shard_map(body, mesh=mesh, in_specs=in_specs, out_specs=out_specs, check_vma=False)
```

```python
import math

import jax
import jax.numpy as jnp
from jax import lax
from jax.experimental import pallas as pl
from jax.experimental.pallas import tpu as pltpu
from jax.sharding import PartitionSpec as P

HEADS = 20
HEAD_DIM = 64


def split_heads(matrix):
    return matrix.reshape(matrix.shape[0], HEADS, HEAD_DIM)


def block_size(rows):
    return math.gcd(rows, 512)


def absorb_block(running, key_rows, value_rows, query_heads, cotan_heads):
    score_scale = HEAD_DIM ** (-0.5)
    highest, summed_weights, weighted_sum = running
    key_heads = split_heads(key_rows)
    value_heads = split_heads(value_rows)
    scores = score_scale * jnp.einsum(
        "qhe,khe->hqk", query_heads, key_heads, preferred_element_type=jnp.float32
    )
    products = jnp.einsum(
        "qhe,khe->hqk", cotan_heads, value_heads, preferred_element_type=jnp.float32
    )
    new_high = jnp.maximum(highest, jnp.max(scores, -1))
    shrink = jnp.exp(highest - new_high)
    weights = jnp.exp(scores - new_high[..., None])
    summed_weights = summed_weights * shrink + jnp.sum(weights, -1)
    weighted_sum = weighted_sum * shrink + jnp.sum(weights * products, -1)
    return (new_high, summed_weights, weighted_sum)


def absorb(running, key_rows, value_rows, query_heads, cotan_heads):
    rows = key_rows.shape[0]
    width = block_size(rows)
    count = rows // width

    def absorb_one(state, pair):
        return (absorb_block(state, pair[0], pair[1], query_heads, cotan_heads), None)

    running, unused = lax.scan(
        absorb_one,
        running,
        (key_rows.reshape(count, width, -1), value_rows.reshape(count, width, -1)),
    )
    return running


def query_block_terms(running, key_rows, value_rows, query_heads, cotan_heads, log_total):
    score_scale = HEAD_DIM ** (-0.5)
    first_sum, second_sum = running
    key_heads = split_heads(key_rows)
    value_heads = split_heads(value_rows)
    scores = score_scale * jnp.einsum(
        "qhe,khe->hqk", query_heads, key_heads, preferred_element_type=jnp.float32
    )
    probabilities = jnp.exp(scores - log_total[..., None])
    products = jnp.einsum(
        "qhe,khe->hqk", cotan_heads, value_heads, preferred_element_type=jnp.float32
    )
    first_sum = first_sum + jnp.einsum(
        "hqk,khe->hqe",
        (probabilities * products).astype(jnp.bfloat16),
        key_heads,
        preferred_element_type=jnp.float32,
    )
    second_sum = second_sum + jnp.einsum(
        "hqk,khe->hqe",
        probabilities.astype(jnp.bfloat16),
        key_heads,
        preferred_element_type=jnp.float32,
    )
    return (first_sum, second_sum)


def query_terms(running, key_rows, value_rows, query_heads, cotan_heads, log_total):
    rows = key_rows.shape[0]
    width = block_size(rows)
    count = rows // width

    def query_one(state, pair):
        return (
            query_block_terms(state, pair[0], pair[1], query_heads, cotan_heads, log_total),
            None,
        )

    running, unused = lax.scan(
        query_one,
        running,
        (key_rows.reshape(count, width, -1), value_rows.reshape(count, width, -1)),
    )
    return running


def key_block_terms(query_heads, cotan_heads, log_total, grad_dot, key_rows, value_rows):
    score_scale = HEAD_DIM ** (-0.5)
    key_heads = split_heads(key_rows)
    value_heads = split_heads(value_rows)
    scores = score_scale * jnp.einsum(
        "qhe,khe->hqk", query_heads, key_heads, preferred_element_type=jnp.float32
    )
    probabilities = jnp.exp(scores - log_total[..., None])
    products = jnp.einsum(
        "qhe,khe->hqk", cotan_heads, value_heads, preferred_element_type=jnp.float32
    )
    slopes = (probabilities * (products - grad_dot[..., None])).astype(jnp.bfloat16)
    key_grads = score_scale * jnp.einsum(
        "hqk,qhe->khe", slopes, query_heads, preferred_element_type=jnp.float32
    )
    value_grads = jnp.einsum(
        "hqk,qhe->khe",
        probabilities.astype(jnp.bfloat16),
        cotan_heads,
        preferred_element_type=jnp.float32,
    )
    return (key_grads.reshape(key_rows.shape[0], -1), value_grads.reshape(key_rows.shape[0], -1))


def key_terms(query_heads, cotan_heads, log_total, grad_dot, key_rows, value_rows):
    rows = query_heads.shape[0]
    width = block_size(rows)
    count = rows // width
    heads_count = log_total.shape[0]
    zero_grads = jnp.zeros((key_rows.shape[0], key_rows.shape[1]), jnp.float32)
    log_blocks = jnp.transpose(log_total.reshape(heads_count, count, width), (1, 0, 2))
    dot_blocks = jnp.transpose(grad_dot.reshape(heads_count, count, width), (1, 0, 2))

    def key_one(state, group):
        key_grads, value_grads = key_block_terms(
            group[0], group[1], group[2], group[3], key_rows, value_rows
        )
        return ((state[0] + key_grads, state[1] + value_grads), None)

    totals, unused = lax.scan(
        key_one,
        (zero_grads, zero_grads),
        (
            query_heads.reshape(count, width, HEADS, HEAD_DIM),
            cotan_heads.reshape(count, width, HEADS, HEAD_DIM),
            log_blocks,
            dot_blocks,
        ),
    )
    return totals


def local(queries, image_keys, image_values, out_grad, text_keys, text_values, reward_ranks):
    row_count = queries.shape[0]
    features = queries.shape[1]
    images_count = reward_ranks.shape[0]
    picked = jnp.sum(
        jnp.where(jnp.arange(images_count) == lax.axis_index("grp"), reward_ranks, 0)
    ).astype(jnp.float32)
    advantage = (picked - 0.5 * (images_count - 1)) / math.sqrt(
        (images_count * images_count - 1) / 12.0
    )
    cotangent = (advantage * out_grad.astype(jnp.float32)).astype(jnp.bfloat16)
    query_heads = split_heads(queries)
    cotan_heads = split_heads(cotangent)
    flat_zero = jnp.zeros((HEADS, row_count), jnp.float32)
    wide_zero = jnp.zeros((HEADS, row_count, HEAD_DIM), jnp.float32)
    start_state = (jnp.full((HEADS, row_count), -1e30, jnp.float32), flat_zero, flat_zero)
    whole_text = (
        lax.all_gather(text_keys, "seq", axis=0, tiled=True),
        lax.all_gather(text_values, "seq", axis=0, tiled=True),
    )
    running = absorb(start_state, whole_text[0], whole_text[1], query_heads, cotan_heads)
    pieces = (
        lax.all_gather(image_keys, "seq", axis=0, tiled=True),
        lax.all_gather(image_values, "seq", axis=0, tiled=True),
    )
    running = absorb(running, pieces[0], pieces[1], query_heads, cotan_heads)
    highest, summed_weights, weighted_sum = running
    log_total = highest + jnp.log(summed_weights)
    grad_dot = weighted_sum / summed_weights
    text_state = query_terms(
        (wide_zero, wide_zero), whole_text[0], whole_text[1], query_heads, cotan_heads, log_total
    )
    pieces = (
        lax.all_gather(image_keys, "seq", axis=0, tiled=True),
        lax.all_gather(image_values, "seq", axis=0, tiled=True),
    )
    first_sum, second_sum = query_terms(
        text_state, pieces[0], pieces[1], query_heads, cotan_heads, log_total
    )
    grad_query = HEAD_DIM ** (-0.5) * (first_sum - grad_dot[..., None] * second_sum)
    grad_queries = (
        jnp.transpose(grad_query, (1, 0, 2)).reshape(row_count, features).astype(jnp.bfloat16)
    )
    all_logs, all_dots = (
        lax.all_gather(log_total.T, "seq", axis=0, tiled=True),
        lax.all_gather(grad_dot.T, "seq", axis=0, tiled=True),
    )
    pieces = (
        lax.all_gather(queries, "seq", axis=0, tiled=True),
        lax.all_gather(cotangent, "seq", axis=0, tiled=True),
    )
    visiting_queries = split_heads(pieces[0])
    visiting_cotans = split_heads(pieces[1])
    key_grads, value_grads = key_terms(
        visiting_queries, visiting_cotans, all_logs.T, all_dots.T, image_keys, image_values
    )
    grad_keys = key_grads.astype(jnp.bfloat16)
    grad_values = value_grads.astype(jnp.bfloat16)
    text_key_part, text_value_part = key_terms(
        query_heads, cotan_heads, log_total, grad_dot, whole_text[0], whole_text[1]
    )
    summed = lax.psum((text_key_part, text_value_part), ("grp", "seq"))
    owned_rows = text_keys.shape[0]
    offset = lax.axis_index("seq") * owned_rows
    text_key_sum = lax.dynamic_slice_in_dim(summed[0], offset, owned_rows, 0)
    text_value_sum = lax.dynamic_slice_in_dim(summed[1], offset, owned_rows, 0)
    return (
        grad_queries,
        grad_keys,
        grad_values,
        text_key_sum.astype(jnp.bfloat16),
        text_value_sum.astype(jnp.bfloat16),
    )


CHIPS = 4
LANES = 128
TILE = 256
MESH = pl.DeviceIdType.MESH
F32 = jnp.float32
BF16 = jnp.bfloat16


def low_lanes(rows):
    return lax.broadcasted_iota(jnp.int32, (rows, LANES), 1) < HEAD_DIM


def swapped(x):
    return pltpu.roll(x.astype(F32), HEAD_DIM, 1)


def pack_head(low, top, bottom):
    mask = low_lanes(top.shape[0])
    if low:
        return jnp.where(mask, top.astype(F32), swapped(bottom))
    return jnp.where(mask, swapped(top), bottom.astype(F32))


def fused(
    ranks, q_in, k_in, v_in, g_in, tk_in, tv_in,
    dq_out, dk_out, dv_out, dtk_out, dtv_out,
    send_a, send_c, recv_a, recv_c, sib_a, sib_c,
    qs, gs, ks, vs, kt, dqs, acc, sib_acc,
    osend_a, osend_c, orecv_a, orecv_c,
    tsend, tterm_a, tterm_c, tz_a, tz_c, tshare, tzr_c, tpiece, tgot,
    in_s, in_r, sib_s, sib_r, acc_s, acc_r, out_s, out_r, grp_s, grp_r, tz_s, tz_r, share_s, share_r, ti_s, ti_r, tf_s, tf_r,
):
    rows = q_in.shape[0]
    text = tk_in.shape[0]
    images = ranks.shape[0]
    grp = lax.axis_index("grp")
    seq = lax.axis_index("seq")
    z = seq // 2
    core = seq % 2

    def peer(step):
        there = (z + step) % CHIPS
        return there, {"seq": there * 2 + core}

    def friend(step):
        there = (grp + step) % images
        return there, {"grp": there}

    sibling = {"seq": z * 2 + 1 - core}

    barrier = pltpu.get_barrier_semaphore()
    for step in range(1, CHIPS):
        pl.semaphore_signal(barrier, inc=1, device_id=peer(step)[1], device_id_type=MESH)
    for step in range(1, images):
        pl.semaphore_signal(barrier, inc=1, device_id=friend(step)[1], device_id_type=MESH)
    pl.semaphore_signal(barrier, inc=1, device_id=sibling, device_id_type=MESH)

    rank = ranks[grp].astype(F32)
    advantage = (jnp.full((1, LANES), rank) - 0.5 * (images - 1)) / math.sqrt(
        (images * images - 1) / 12.0
    )

    def cotangent(columns):
        return (advantage * g_in[:, columns].astype(F32)).astype(BF16)

    def part(t, pair_ref, single_ref):
        return pair_ref.at[t] if t < 2 else single_ref

    sizes = [(rows, text), (rows, text), (rows // 2, text // 2)]

    def pack(t):
        r, n = sizes[t]
        dst = part(t, send_a, send_c)
        for chip in range(CHIPS):
            if t < 2:
                cols = slice((2 * chip + t) * LANES, (2 * chip + t + 1) * LANES)
                pieces = [q_in[:, cols], cotangent(cols), k_in[:, cols], v_in[:, cols]]
            else:
                cols = slice((8 + chip // 2) * LANES, (9 + chip // 2) * LANES)
                whole = [
                    q_in[:, cols], cotangent(cols), k_in[:, cols], v_in[:, cols],
                    tk_in[:, cols], tv_in[:, cols],
                ]
                pieces = []
                for x in whole:
                    half = x.shape[0] // 2
                    x = x.astype(F32)
                    pieces.append(pack_head(chip % 2 == 0, x[:half], x[half:]).astype(BF16))
            at = 0
            for x in pieces:
                dst[chip, at : at + x.shape[0], :] = x
                at += x.shape[0]
        if t < 2:
            recv_a[t, z, 0 : 4 * rows, :] = send_a[t, z, 0 : 4 * rows, :]
        else:
            recv_c[z] = send_c[z]

    share = 2 * text // images

    def pack_text(t):
        for chip in range(CHIPS):
            cols = slice((2 * chip + t) * LANES, (2 * chip + t + 1) * LANES)
            for which, x in ((0, tk_in), (1, tv_in)):
                for j in range(images // 2):
                    tpiece[t, which * (images // 2) + j, chip] = x[
                        j * share : (j + 1) * share, cols
                    ]
        tgot[t, grp, z] = tpiece[t, grp, z]

    def text_copy(t, step):
        there, device = peer(step)
        return pltpu.make_async_remote_copy(
            src_ref=tpiece.at[t, grp, there],
            dst_ref=tgot.at[t, grp, z],
            send_sem=ti_s.at[t, step],
            recv_sem=ti_r.at[t, step],
            device_id=device,
            device_id_type=MESH,
        )

    def spread_copy(t, step):
        there, device = friend(step)
        return pltpu.make_async_remote_copy(
            src_ref=tgot.at[t, grp],
            dst_ref=tgot.at[t, grp],
            send_sem=tf_s.at[t, step],
            recv_sem=tf_r.at[t, step],
            device_id=device,
            device_id_type=MESH,
        )

    def in_copy(t, step):
        there, device = peer(step)
        if t < 2:
            image_rows = pl.ds(0, 4 * rows)
            return pltpu.make_async_remote_copy(
                src_ref=send_a.at[t, there, image_rows, :],
                dst_ref=recv_a.at[t, z, image_rows, :],
                send_sem=in_s.at[t, step],
                recv_sem=in_r.at[t, step],
                device_id=device,
                device_id_type=MESH,
            )
        return pltpu.make_async_remote_copy(
            src_ref=part(t, send_a, send_c).at[there],
            dst_ref=part(t, recv_a, recv_c).at[z],
            send_sem=in_s.at[t, step],
            recv_sem=in_r.at[t, step],
            device_id=device,
            device_id_type=MESH,
        )

    def sib_copy(t):
        r, n = sizes[t]
        return pltpu.make_async_remote_copy(
            src_ref=part(t, recv_a, recv_c).at[:, pl.ds(2 * r, 2 * r + 2 * n), :],
            dst_ref=part(t, sib_a, sib_c),
            send_sem=sib_s.at[t],
            recv_sem=sib_r.at[t],
            device_id=sibling,
            device_id_type=MESH,
        )

    half_keys = CHIPS * (rows + text)
    queries = CHIPS * rows

    def acc_copy(t):
        return pltpu.make_async_remote_copy(
            src_ref=acc.at[t, :, pl.ds(half_keys, half_keys), :],
            dst_ref=sib_acc.at[t],
            send_sem=acc_s.at[t],
            recv_sem=acc_r.at[t],
            device_id=sibling,
            device_id_type=MESH,
        )

    def out_copy(t, step):
        there, device = peer(step)
        return pltpu.make_async_remote_copy(
            src_ref=part(t, osend_a, osend_c).at[there],
            dst_ref=part(t, orecv_a, orecv_c).at[z],
            send_sem=out_s.at[t, step],
            recv_sem=out_r.at[t, step],
            device_id=device,
            device_id_type=MESH,
        )

    def grp_copy(t, step):
        there, device = friend(step)
        if t < 2:
            src = tsend.at[t, there]
            dst = tterm_a.at[t, grp]
        else:
            src = tterm_c.at[grp]
            dst = tterm_c.at[grp]
        return pltpu.make_async_remote_copy(
            src_ref=src,
            dst_ref=dst,
            send_sem=grp_s.at[t, step],
            recv_sem=grp_r.at[t, step],
            device_id=device,
            device_id_type=MESH,
        )

    def share_copy(t, step):
        there, device = friend(step)
        return pltpu.make_async_remote_copy(
            src_ref=tshare.at[t, grp],
            dst_ref=tshare.at[t, grp],
            send_sem=share_s.at[t, step],
            recv_sem=share_r.at[t, step],
            device_id=device,
            device_id_type=MESH,
        )

    def tz_copy(t, step):
        there, device = peer(step)
        return pltpu.make_async_remote_copy(
            src_ref=(tz_a.at[t] if t < 2 else tz_c).at[there],
            dst_ref=tshare.at[t, grp, z] if t < 2 else tzr_c.at[z],
            send_sem=tz_s.at[t, step],
            recv_sem=tz_r.at[t, step],
            device_id=device,
            device_id_type=MESH,
        )

    for t in range(2):
        pack_text(t)
    pack(0)
    pl.semaphore_wait(barrier, CHIPS - 1 + images - 1 + 1)
    for t in range(2):
        for step in range(1, CHIPS):
            text_copy(t, step).start()
    for t in range(3):
        if t > 0:
            pack(t)
        for step in range(1, CHIPS):
            in_copy(t, step).start()

    for t in range(2):
        for step in range(1, CHIPS):
            text_copy(t, step).wait_recv()
        for step in range(1, images):
            spread_copy(t, step).start()

    factor = HEAD_DIM ** (-0.5) * math.log2(math.e)

    def gathered(x):
        return x.reshape(x.shape[0] * x.shape[1], LANES)

    def unpacked(x):
        return jnp.concatenate([x.astype(F32), swapped(x)], 0).astype(BF16)

    def load_queries(t):
        r, n = sizes[t]
        src = part(t, recv_a, recv_c)
        for dst, at in ((qs, 0), (gs, r)):
            x = gathered(src[:, at : at + r, :])
            mask = low_lanes(queries)
            if t < 2:
                dst[0:queries] = jnp.where(mask, x, jnp.zeros_like(x))
                dst[queries : 2 * queries] = jnp.where(mask, jnp.zeros_like(x), x)
            else:
                x = unpacked(x)
                dst[0:queries] = jnp.where(mask, x, jnp.zeros_like(x))

    def load_keys(t, source, base, at):
        r, n = sizes[t]
        for dst, shift, text_at in ((ks, 0, 2 * r), (vs, r, 2 * r + n)):
            x = gathered(
                jnp.concatenate(
                    [
                        source[:, at + shift : at + shift + r, :],
                        source[:, at + text_at : at + text_at + n, :],
                    ],
                    1,
                )
            )
            if t == 2:
                x = unpacked(x)
            dst[base : base + half_keys] = x

    def compute(t):
        heads = 2 if t < 2 else 1
        acc[t] = jnp.zeros(acc.shape[1:], F32)
        kt[...] = ks[...].astype(F32).T.astype(BF16)

        def body(i, carry):
            place = pl.ds(pl.multiple_of(i * TILE, TILE), TILE)
            q = qs[place, :]
            g = gs[place, :]
            nt = (((1,), (1,)), ((), ()))
            s = lax.dot_general(ks[...], q, nt, preferred_element_type=F32)
            dp = lax.dot_general(vs[...], g, nt, preferred_element_type=F32)
            e = jnp.exp2((s - jnp.max(s, 0, keepdims=True)) * factor)
            inverse = 1.0 / jnp.sum(e, 0, keepdims=True)
            p = e * inverse
            dot = jnp.sum(p * dp, 0, keepdims=True)
            slopes = (p * (dp - dot)).astype(BF16)
            acc[t, 0] += jnp.dot(slopes, q, preferred_element_type=F32)
            acc[t, 1] += jnp.dot(p.astype(BF16), g, preferred_element_type=F32)
            dqs[place, :] = jnp.dot(kt[...], slopes, preferred_element_type=F32).T
            return carry

        lax.fori_loop(0, heads * queries // TILE, body, 0)

    scale = HEAD_DIM ** (-0.5)

    def finish(t):
        r, n = sizes[t]
        dst = part(t, osend_a, osend_c)
        mask = low_lanes(queries)
        if t < 2:
            x = jnp.where(mask, dqs[0:queries], dqs[queries : 2 * queries])
        else:
            x = pack_head(True, dqs[0 : queries // 2], dqs[queries // 2 : queries])
        dst[:, 0:r, :] = (scale * x).astype(BF16).reshape(CHIPS, r, LANES)
        acc_copy(t).wait_recv()
        for which in range(2):
            x = acc[t, which, 0:half_keys, :] + sib_acc[t, which]
            if which == 0:
                x = scale * x
            if t == 2:
                x = pack_head(True, x[: half_keys // 2], x[half_keys // 2 :])
            x = x.reshape(CHIPS, r + n, LANES)
            dst[:, (1 + which) * r : (2 + which) * r, :] = x[:, :r].astype(BF16)
            if t < 2:
                half = images // 2
                for j in range(half):
                    tsend[t, which * half + j] = x[:, r + j * share : r + (j + 1) * share]
            else:
                tterm_c[grp, :, which * n : (which + 1) * n, :] = x[:, r:]
        for step in range(1, CHIPS):
            out_copy(t, step).start()
        for step in range(1, images):
            grp_copy(t, step).start()
        if t < 2:
            tterm_a[t, grp] = tsend[t, grp]
        part(t, orecv_a, orecv_c)[z] = dst[z]

    def finish_text(t):
        terms = part(t, tterm_a, tterm_c)
        for step in range(1, images):
            grp_copy(t, step).wait_recv()
        total = terms[0]
        for image in range(1, images):
            total = total + terms[image]
        dst = part(t, tz_a, tz_c)
        dst[...] = total.astype(BF16)
        for step in range(1, CHIPS):
            tz_copy(t, step).start()
        if t < 2:
            tshare[t, grp, z] = dst[z]
        else:
            tzr_c[z] = dst[z]

    def share_text(t):
        for step in range(1, CHIPS):
            tz_copy(t, step).wait_recv()
        for step in range(1, images):
            share_copy(t, step).start()

    def place_out(t):
        r, n = sizes[t]
        src = part(t, orecv_a, orecv_c)
        for step in range(1, CHIPS):
            out_copy(t, step).wait_recv()
        for which, dst in ((0, dq_out), (1, dk_out), (2, dv_out)):
            place(t, src, which * r, r, dst)

    def place_text(t):
        r, n = sizes[t]
        if t < 2:
            for step in range(1, images):
                share_copy(t, step).wait_recv()
            half = images // 2
            for which, dst in ((0, dtk_out), (1, dtv_out)):
                for chip in range(CHIPS):
                    cols = slice((2 * chip + t) * LANES, (2 * chip + t + 1) * LANES)
                    for j in range(half):
                        dst[j * share : (j + 1) * share, cols] = tshare[t, which * half + j, chip]
            return
        for step in range(1, CHIPS):
            tz_copy(t, step).wait_recv()
        for which, dst in ((0, dtk_out), (1, dtv_out)):
            place(t, tzr_c, which * n, n, dst)

    def place(t, src, at, r, dst):
        if t < 2:
            for chip in range(CHIPS):
                cols = slice((2 * chip + t) * LANES, (2 * chip + t + 1) * LANES)
                dst[:, cols] = src[chip, at : at + r, :]
        else:
            for pair in range(2):
                cols = slice((8 + pair) * LANES, (9 + pair) * LANES)
                low = src[2 * pair, at : at + r, :].astype(F32)
                high = src[2 * pair + 1, at : at + r, :].astype(F32)
                mask = low_lanes(r)
                dst[0:r, cols] = jnp.where(mask, low, swapped(high)).astype(BF16)
                dst[r : 2 * r, cols] = jnp.where(mask, swapped(low), high).astype(BF16)

    for t in range(3):
        r, n = sizes[t]
        for step in range(1, CHIPS):
            in_copy(t, step).wait_recv()
        if t < 2:
            for step in range(1, images):
                spread_copy(t, step).wait_recv()
            for j in range(images):
                place_at = 4 * rows + j * share
                recv_a[t, :, place_at : place_at + share, :] = tgot[t, j]
        sib_copy(t).start()
        load_queries(t)
        load_keys(t, part(t, recv_a, recv_c), 0, 2 * r)
        sib_copy(t).wait_recv()
        load_keys(t, part(t, sib_a, sib_c), half_keys, 0)
        compute(t)
        acc_copy(t).start()
        if t > 0:
            finish_text(t - 1)
        finish(t)
    finish_text(2)
    share_text(0)
    share_text(1)
    place_out(0)
    place_text(0)
    place_out(1)
    place_text(1)
    place_out(2)
    place_text(2)
    for t in range(3):
        for step in range(1, CHIPS):
            in_copy(t, step).wait_send()
            if t < 2:
                text_copy(t, step).wait_send()
            out_copy(t, step).wait_send()
            tz_copy(t, step).wait_send()
        for step in range(1, images):
            grp_copy(t, step).wait_send()
            if t < 2:
                share_copy(t, step).wait_send()
                spread_copy(t, step).wait_send()
        sib_copy(t).wait_send()
        acc_copy(t).wait_send()


def write_out(*refs):
    sems = refs[10]
    copies = [pltpu.make_async_copy(refs[i], refs[5 + i], sems.at[i]) for i in range(5)]
    for copy in copies:
        copy.start()
    for copy in copies:
        copy.wait()


def exchange(queries, image_keys, image_values, out_grad, text_keys, text_values, reward_ranks):
    rows = queries.shape[0]
    text = text_keys.shape[0]
    images = reward_ranks.shape[0]
    width = 4 * rows + 2 * text
    keys = 2 * CHIPS * (rows + text)
    asked = CHIPS * rows
    like = lambda x: jax.ShapeDtypeStruct(x.shape, BF16)

    def pair_and_single(count, n, dtype):
        return [
            pltpu.VMEM((2, count, n, LANES), dtype),
            pltpu.VMEM((count, n // 2, LANES), dtype),
        ]

    def text_terms(n):
        return [
            pltpu.VMEM((2, images, CHIPS, n // images, LANES), F32),
            pltpu.VMEM((2, images, CHIPS, n // images, LANES), F32),
            pltpu.VMEM((images, CHIPS, n // 2, LANES), F32),
        ]

    dma = pltpu.SemaphoreType.DMA
    results = pl.pallas_call(
        fused,
        out_shape=[like(x) for x in (queries, image_keys, image_values, text_keys, text_values)],
        in_specs=[pl.BlockSpec(memory_space=pltpu.SMEM)]
        + [pl.BlockSpec(memory_space=pltpu.VMEM)] * 6,
        out_specs=[pl.BlockSpec(memory_space=pltpu.VMEM)] * 5,
        scratch_shapes=pair_and_single(CHIPS, width, BF16)
        + pair_and_single(CHIPS, width, BF16)
        + pair_and_single(CHIPS, 2 * rows + 2 * text, BF16)
        + [
            pltpu.VMEM((2 * asked, LANES), BF16),
            pltpu.VMEM((2 * asked, LANES), BF16),
            pltpu.VMEM((keys, LANES), BF16),
            pltpu.VMEM((keys, LANES), BF16),
            pltpu.VMEM((LANES, keys), BF16),
            pltpu.VMEM((2 * asked, LANES), F32),
            pltpu.VMEM((3, 2, keys, LANES), F32),
            pltpu.VMEM((3, 2, keys // 2, LANES), F32),
        ]
        + pair_and_single(CHIPS, 3 * rows, BF16)
        + pair_and_single(CHIPS, 3 * rows, BF16)
        + text_terms(2 * text)
        + [
            pltpu.VMEM((2, CHIPS, 2 * text // images, LANES), BF16),
            pltpu.VMEM((CHIPS, text, LANES), BF16),
            pltpu.VMEM((2, images, CHIPS, 2 * text // images, LANES), BF16),
            pltpu.VMEM((CHIPS, text, LANES), BF16),
            pltpu.VMEM((2, images, CHIPS, 2 * text // images, LANES), BF16),
            pltpu.VMEM((2, images, CHIPS, 2 * text // images, LANES), BF16),
        ]
        + [dma((3, CHIPS)), dma((3, CHIPS)), dma((3,)), dma((3,)), dma((3,)), dma((3,))]
        + [dma((3, CHIPS)), dma((3, CHIPS)), dma((3, images)), dma((3, images))]
        + [dma((3, CHIPS)), dma((3, CHIPS)), dma((2, images)), dma((2, images))]
        + [dma((2, CHIPS)), dma((2, CHIPS)), dma((2, images)), dma((2, images))],
        compiler_params=pltpu.CompilerParams(
            collective_id=0, has_side_effects=True, vmem_limit_bytes=56 * 1024 * 1024
        ),
    )(reward_ranks, queries, image_keys, image_values, out_grad, text_keys, text_values)
    return pl.pallas_call(
        write_out,
        out_shape=[like(x) for x in results],
        in_specs=[pl.BlockSpec(memory_space=pltpu.VMEM)] * 5,
        out_specs=[pl.BlockSpec(memory_space=pl.ANY)] * 5,
        scratch_shapes=[dma((5,))],
    )(*results)


def solution(mesh):
    in_specs = (
        P(("grp", "seq"), None),
        P(("grp", "seq"), None),
        P(("grp", "seq"), None),
        P(("grp", "seq"), None),
        P("seq", None),
        P("seq", None),
        P(),
    )
    out_specs = (
        P(("grp", "seq"), None),
        P(("grp", "seq"), None),
        P(("grp", "seq"), None),
        P("seq", None),
        P("seq", None),
    )
    body = exchange if mesh.shape["seq"] == 2 * CHIPS else local
    return jax.shard_map(body, mesh=mesh, in_specs=in_specs, out_specs=out_specs, check_vma=False)
```

```python
import math

import jax
import jax.numpy as jnp
from jax import lax
from jax.experimental import pallas as pl
from jax.experimental.pallas import tpu as pltpu
from jax.sharding import PartitionSpec as P

HEADS = 20
HEAD_DIM = 64


def split_heads(matrix):
    return matrix.reshape(matrix.shape[0], HEADS, HEAD_DIM)


def block_size(rows):
    return math.gcd(rows, 512)


def absorb_block(running, key_rows, value_rows, query_heads, cotan_heads):
    score_scale = HEAD_DIM ** (-0.5)
    highest, summed_weights, weighted_sum = running
    key_heads = split_heads(key_rows)
    value_heads = split_heads(value_rows)
    scores = score_scale * jnp.einsum(
        "qhe,khe->hqk", query_heads, key_heads, preferred_element_type=jnp.float32
    )
    products = jnp.einsum(
        "qhe,khe->hqk", cotan_heads, value_heads, preferred_element_type=jnp.float32
    )
    new_high = jnp.maximum(highest, jnp.max(scores, -1))
    shrink = jnp.exp(highest - new_high)
    weights = jnp.exp(scores - new_high[..., None])
    summed_weights = summed_weights * shrink + jnp.sum(weights, -1)
    weighted_sum = weighted_sum * shrink + jnp.sum(weights * products, -1)
    return (new_high, summed_weights, weighted_sum)


def absorb(running, key_rows, value_rows, query_heads, cotan_heads):
    rows = key_rows.shape[0]
    width = block_size(rows)
    count = rows // width

    def absorb_one(state, pair):
        return (absorb_block(state, pair[0], pair[1], query_heads, cotan_heads), None)

    running, unused = lax.scan(
        absorb_one,
        running,
        (key_rows.reshape(count, width, -1), value_rows.reshape(count, width, -1)),
    )
    return running


def query_block_terms(running, key_rows, value_rows, query_heads, cotan_heads, log_total):
    score_scale = HEAD_DIM ** (-0.5)
    first_sum, second_sum = running
    key_heads = split_heads(key_rows)
    value_heads = split_heads(value_rows)
    scores = score_scale * jnp.einsum(
        "qhe,khe->hqk", query_heads, key_heads, preferred_element_type=jnp.float32
    )
    probabilities = jnp.exp(scores - log_total[..., None])
    products = jnp.einsum(
        "qhe,khe->hqk", cotan_heads, value_heads, preferred_element_type=jnp.float32
    )
    first_sum = first_sum + jnp.einsum(
        "hqk,khe->hqe",
        (probabilities * products).astype(jnp.bfloat16),
        key_heads,
        preferred_element_type=jnp.float32,
    )
    second_sum = second_sum + jnp.einsum(
        "hqk,khe->hqe",
        probabilities.astype(jnp.bfloat16),
        key_heads,
        preferred_element_type=jnp.float32,
    )
    return (first_sum, second_sum)


def query_terms(running, key_rows, value_rows, query_heads, cotan_heads, log_total):
    rows = key_rows.shape[0]
    width = block_size(rows)
    count = rows // width

    def query_one(state, pair):
        return (
            query_block_terms(state, pair[0], pair[1], query_heads, cotan_heads, log_total),
            None,
        )

    running, unused = lax.scan(
        query_one,
        running,
        (key_rows.reshape(count, width, -1), value_rows.reshape(count, width, -1)),
    )
    return running


def key_block_terms(query_heads, cotan_heads, log_total, grad_dot, key_rows, value_rows):
    score_scale = HEAD_DIM ** (-0.5)
    key_heads = split_heads(key_rows)
    value_heads = split_heads(value_rows)
    scores = score_scale * jnp.einsum(
        "qhe,khe->hqk", query_heads, key_heads, preferred_element_type=jnp.float32
    )
    probabilities = jnp.exp(scores - log_total[..., None])
    products = jnp.einsum(
        "qhe,khe->hqk", cotan_heads, value_heads, preferred_element_type=jnp.float32
    )
    slopes = (probabilities * (products - grad_dot[..., None])).astype(jnp.bfloat16)
    key_grads = score_scale * jnp.einsum(
        "hqk,qhe->khe", slopes, query_heads, preferred_element_type=jnp.float32
    )
    value_grads = jnp.einsum(
        "hqk,qhe->khe",
        probabilities.astype(jnp.bfloat16),
        cotan_heads,
        preferred_element_type=jnp.float32,
    )
    return (key_grads.reshape(key_rows.shape[0], -1), value_grads.reshape(key_rows.shape[0], -1))


def key_terms(query_heads, cotan_heads, log_total, grad_dot, key_rows, value_rows):
    rows = query_heads.shape[0]
    width = block_size(rows)
    count = rows // width
    heads_count = log_total.shape[0]
    zero_grads = jnp.zeros((key_rows.shape[0], key_rows.shape[1]), jnp.float32)
    log_blocks = jnp.transpose(log_total.reshape(heads_count, count, width), (1, 0, 2))
    dot_blocks = jnp.transpose(grad_dot.reshape(heads_count, count, width), (1, 0, 2))

    def key_one(state, group):
        key_grads, value_grads = key_block_terms(
            group[0], group[1], group[2], group[3], key_rows, value_rows
        )
        return ((state[0] + key_grads, state[1] + value_grads), None)

    totals, unused = lax.scan(
        key_one,
        (zero_grads, zero_grads),
        (
            query_heads.reshape(count, width, HEADS, HEAD_DIM),
            cotan_heads.reshape(count, width, HEADS, HEAD_DIM),
            log_blocks,
            dot_blocks,
        ),
    )
    return totals


def local(queries, image_keys, image_values, out_grad, text_keys, text_values, reward_ranks):
    row_count = queries.shape[0]
    features = queries.shape[1]
    images_count = reward_ranks.shape[0]
    picked = jnp.sum(
        jnp.where(jnp.arange(images_count) == lax.axis_index("grp"), reward_ranks, 0)
    ).astype(jnp.float32)
    advantage = (picked - 0.5 * (images_count - 1)) / math.sqrt(
        (images_count * images_count - 1) / 12.0
    )
    cotangent = (advantage * out_grad.astype(jnp.float32)).astype(jnp.bfloat16)
    query_heads = split_heads(queries)
    cotan_heads = split_heads(cotangent)
    flat_zero = jnp.zeros((HEADS, row_count), jnp.float32)
    wide_zero = jnp.zeros((HEADS, row_count, HEAD_DIM), jnp.float32)
    start_state = (jnp.full((HEADS, row_count), -1e30, jnp.float32), flat_zero, flat_zero)
    whole_text = (
        lax.all_gather(text_keys, "seq", axis=0, tiled=True),
        lax.all_gather(text_values, "seq", axis=0, tiled=True),
    )
    running = absorb(start_state, whole_text[0], whole_text[1], query_heads, cotan_heads)
    pieces = (
        lax.all_gather(image_keys, "seq", axis=0, tiled=True),
        lax.all_gather(image_values, "seq", axis=0, tiled=True),
    )
    running = absorb(running, pieces[0], pieces[1], query_heads, cotan_heads)
    highest, summed_weights, weighted_sum = running
    log_total = highest + jnp.log(summed_weights)
    grad_dot = weighted_sum / summed_weights
    text_state = query_terms(
        (wide_zero, wide_zero), whole_text[0], whole_text[1], query_heads, cotan_heads, log_total
    )
    pieces = (
        lax.all_gather(image_keys, "seq", axis=0, tiled=True),
        lax.all_gather(image_values, "seq", axis=0, tiled=True),
    )
    first_sum, second_sum = query_terms(
        text_state, pieces[0], pieces[1], query_heads, cotan_heads, log_total
    )
    grad_query = HEAD_DIM ** (-0.5) * (first_sum - grad_dot[..., None] * second_sum)
    grad_queries = (
        jnp.transpose(grad_query, (1, 0, 2)).reshape(row_count, features).astype(jnp.bfloat16)
    )
    all_logs, all_dots = (
        lax.all_gather(log_total.T, "seq", axis=0, tiled=True),
        lax.all_gather(grad_dot.T, "seq", axis=0, tiled=True),
    )
    pieces = (
        lax.all_gather(queries, "seq", axis=0, tiled=True),
        lax.all_gather(cotangent, "seq", axis=0, tiled=True),
    )
    visiting_queries = split_heads(pieces[0])
    visiting_cotans = split_heads(pieces[1])
    key_grads, value_grads = key_terms(
        visiting_queries, visiting_cotans, all_logs.T, all_dots.T, image_keys, image_values
    )
    grad_keys = key_grads.astype(jnp.bfloat16)
    grad_values = value_grads.astype(jnp.bfloat16)
    text_key_part, text_value_part = key_terms(
        query_heads, cotan_heads, log_total, grad_dot, whole_text[0], whole_text[1]
    )
    summed = lax.psum((text_key_part, text_value_part), ("grp", "seq"))
    owned_rows = text_keys.shape[0]
    offset = lax.axis_index("seq") * owned_rows
    text_key_sum = lax.dynamic_slice_in_dim(summed[0], offset, owned_rows, 0)
    text_value_sum = lax.dynamic_slice_in_dim(summed[1], offset, owned_rows, 0)
    return (
        grad_queries,
        grad_keys,
        grad_values,
        text_key_sum.astype(jnp.bfloat16),
        text_value_sum.astype(jnp.bfloat16),
    )


CHIPS = 4
LANES = 128
TILE = 256
MESH = pl.DeviceIdType.MESH
F32 = jnp.float32
BF16 = jnp.bfloat16


def low_lanes(rows):
    return lax.broadcasted_iota(jnp.int32, (rows, LANES), 1) < HEAD_DIM


def swapped(x):
    return pltpu.roll(x.astype(F32), HEAD_DIM, 1)


def pack_head(low, top, bottom):
    mask = low_lanes(top.shape[0])
    if low:
        return jnp.where(mask, top.astype(F32), swapped(bottom))
    return jnp.where(mask, swapped(top), bottom.astype(F32))


def fused(
    ranks, q_in, k_in, v_in, g_in, tk_in, tv_in,
    dq_out, dk_out, dv_out, dtk_out, dtv_out,
    send_a, send_c, recv_a, recv_c, sib_a, sib_c,
    qs, gs, ks, vs, kt, dqs, acc, sib_acc,
    osend_a, osend_c, orecv_a, orecv_c,
    tsend, tterm_a, tterm_c, tz_a, tz_c, tshare, tzr_c, tpiece, tgot,
    in_s, in_r, sib_s, sib_r, acc_s, acc_r, out_s, out_r, grp_s, grp_r, tz_s, tz_r, share_s, share_r, ti_s, ti_r, tf_s, tf_r,
):
    rows = q_in.shape[0]
    text = tk_in.shape[0]
    images = ranks.shape[0]
    grp = lax.axis_index("grp")
    seq = lax.axis_index("seq")
    z = seq // 2
    core = seq % 2

    def peer(step):
        there = (z + step) % CHIPS
        return there, {"seq": there * 2 + core}

    def friend(step):
        there = (grp + step) % images
        return there, {"grp": there}

    sibling = {"seq": z * 2 + 1 - core}

    barrier = pltpu.get_barrier_semaphore()
    for step in range(1, CHIPS):
        pl.semaphore_signal(barrier, inc=1, device_id=peer(step)[1], device_id_type=MESH)
    for step in range(1, images):
        pl.semaphore_signal(barrier, inc=1, device_id=friend(step)[1], device_id_type=MESH)
    pl.semaphore_signal(barrier, inc=1, device_id=sibling, device_id_type=MESH)

    rank = ranks[grp].astype(F32)
    advantage = (jnp.full((1, LANES), rank) - 0.5 * (images - 1)) / math.sqrt(
        (images * images - 1) / 12.0
    )

    def cotangent(columns):
        return (advantage * g_in[:, columns].astype(F32)).astype(BF16)

    def part(t, pair_ref, single_ref):
        return pair_ref.at[t] if t < 2 else single_ref

    sizes = [(rows, text), (rows, text), (rows // 2, text // 2)]

    def pack(t):
        r, n = sizes[t]
        dst = part(t, send_a, send_c)
        for chip in range(CHIPS):
            if t < 2:
                cols = slice((2 * chip + t) * LANES, (2 * chip + t + 1) * LANES)
                pieces = [q_in[:, cols], cotangent(cols), k_in[:, cols], v_in[:, cols]]
            else:
                cols = slice((8 + chip // 2) * LANES, (9 + chip // 2) * LANES)
                whole = [
                    q_in[:, cols], cotangent(cols), k_in[:, cols], v_in[:, cols],
                    tk_in[:, cols], tv_in[:, cols],
                ]
                pieces = []
                for x in whole:
                    half = x.shape[0] // 2
                    x = x.astype(F32)
                    pieces.append(pack_head(chip % 2 == 0, x[:half], x[half:]).astype(BF16))
            at = 0
            for x in pieces:
                dst[chip, at : at + x.shape[0], :] = x
                at += x.shape[0]
        if t < 2:
            recv_a[t, z, 0 : 4 * rows, :] = send_a[t, z, 0 : 4 * rows, :]
        else:
            recv_c[z] = send_c[z]

    share = 2 * text // images

    def pack_text(t):
        for chip in range(CHIPS):
            cols = slice((2 * chip + t) * LANES, (2 * chip + t + 1) * LANES)
            for which, x in ((0, tk_in), (1, tv_in)):
                for j in range(images // 2):
                    tpiece[t, which * (images // 2) + j, chip] = x[
                        j * share : (j + 1) * share, cols
                    ]
        tgot[t, grp, z] = tpiece[t, grp, z]

    def text_copy(t, step):
        there, device = peer(step)
        return pltpu.make_async_remote_copy(
            src_ref=tpiece.at[t, grp, there],
            dst_ref=tgot.at[t, grp, z],
            send_sem=ti_s.at[t, step],
            recv_sem=ti_r.at[t, step],
            device_id=device,
            device_id_type=MESH,
        )

    def spread_copy(t, step):
        there, device = friend(step)
        return pltpu.make_async_remote_copy(
            src_ref=tgot.at[t, grp],
            dst_ref=tgot.at[t, grp],
            send_sem=tf_s.at[t, step],
            recv_sem=tf_r.at[t, step],
            device_id=device,
            device_id_type=MESH,
        )

    def in_copy(t, step):
        there, device = peer(step)
        if t < 2:
            image_rows = pl.ds(0, 4 * rows)
            return pltpu.make_async_remote_copy(
                src_ref=send_a.at[t, there, image_rows, :],
                dst_ref=recv_a.at[t, z, image_rows, :],
                send_sem=in_s.at[t, step],
                recv_sem=in_r.at[t, step],
                device_id=device,
                device_id_type=MESH,
            )
        return pltpu.make_async_remote_copy(
            src_ref=part(t, send_a, send_c).at[there],
            dst_ref=part(t, recv_a, recv_c).at[z],
            send_sem=in_s.at[t, step],
            recv_sem=in_r.at[t, step],
            device_id=device,
            device_id_type=MESH,
        )

    def sib_copy(t):
        r, n = sizes[t]
        return pltpu.make_async_remote_copy(
            src_ref=part(t, recv_a, recv_c).at[:, pl.ds(2 * r, 2 * r + 2 * n), :],
            dst_ref=part(t, sib_a, sib_c),
            send_sem=sib_s.at[t],
            recv_sem=sib_r.at[t],
            device_id=sibling,
            device_id_type=MESH,
        )

    half_keys = CHIPS * (rows + text)
    queries = CHIPS * rows

    def acc_copy(t):
        count = half_keys if t < 2 else half_keys // 2
        return pltpu.make_async_remote_copy(
            src_ref=acc.at[t, :, pl.ds(half_keys, count), :],
            dst_ref=sib_acc.at[t, :, pl.ds(0, count), :],
            send_sem=acc_s.at[t],
            recv_sem=acc_r.at[t],
            device_id=sibling,
            device_id_type=MESH,
        )

    def out_copy(t, step):
        there, device = peer(step)
        return pltpu.make_async_remote_copy(
            src_ref=part(t, osend_a, osend_c).at[there],
            dst_ref=part(t, orecv_a, orecv_c).at[z],
            send_sem=out_s.at[t, step],
            recv_sem=out_r.at[t, step],
            device_id=device,
            device_id_type=MESH,
        )

    def grp_copy(t, step):
        there, device = friend(step)
        if t < 2:
            src = tsend.at[t, there]
            dst = tterm_a.at[t, grp]
        else:
            src = tterm_c.at[grp]
            dst = tterm_c.at[grp]
        return pltpu.make_async_remote_copy(
            src_ref=src,
            dst_ref=dst,
            send_sem=grp_s.at[t, step],
            recv_sem=grp_r.at[t, step],
            device_id=device,
            device_id_type=MESH,
        )

    def share_copy(t, step):
        there, device = friend(step)
        return pltpu.make_async_remote_copy(
            src_ref=tshare.at[t, grp],
            dst_ref=tshare.at[t, grp],
            send_sem=share_s.at[t, step],
            recv_sem=share_r.at[t, step],
            device_id=device,
            device_id_type=MESH,
        )

    def tz_copy(t, step):
        there, device = peer(step)
        return pltpu.make_async_remote_copy(
            src_ref=(tz_a.at[t] if t < 2 else tz_c).at[there],
            dst_ref=tshare.at[t, grp, z] if t < 2 else tzr_c.at[z],
            send_sem=tz_s.at[t, step],
            recv_sem=tz_r.at[t, step],
            device_id=device,
            device_id_type=MESH,
        )

    for t in range(2):
        pack_text(t)
    pack(0)
    pl.semaphore_wait(barrier, CHIPS - 1 + images - 1 + 1)
    for t in range(2):
        for step in range(1, CHIPS):
            text_copy(t, step).start()
    for t in range(3):
        if t > 0:
            pack(t)
        for step in range(1, CHIPS):
            in_copy(t, step).start()

    for t in range(2):
        for step in range(1, CHIPS):
            text_copy(t, step).wait_recv()
        for step in range(1, images):
            spread_copy(t, step).start()

    factor = HEAD_DIM ** (-0.5) * math.log2(math.e)

    def gathered(x):
        return x.reshape(x.shape[0] * x.shape[1], LANES)

    def unpacked(x):
        return jnp.concatenate([x.astype(F32), swapped(x)], 0).astype(BF16)

    def load_queries(t):
        r, n = sizes[t]
        src = part(t, recv_a, recv_c)
        for dst, at in ((qs, 0), (gs, r)):
            x = gathered(src[:, at : at + r, :])
            mask = low_lanes(queries)
            if t < 2:
                dst[0:queries] = jnp.where(mask, x, jnp.zeros_like(x))
                dst[queries : 2 * queries] = jnp.where(mask, jnp.zeros_like(x), x)
            else:
                x = unpacked(x)
                dst[0:queries] = jnp.where(mask, x, jnp.zeros_like(x))

    def load_keys(t, source, base, at):
        r, n = sizes[t]
        for dst, shift, text_at in ((ks, 0, 2 * r), (vs, r, 2 * r + n)):
            x = gathered(
                jnp.concatenate(
                    [
                        source[:, at + shift : at + shift + r, :],
                        source[:, at + text_at : at + text_at + n, :],
                    ],
                    1,
                )
            )
            if t == 2:
                x = unpacked(x)
            dst[base : base + half_keys] = x

    def compute(t):
        heads = 2 if t < 2 else 1
        acc[t] = jnp.zeros(acc.shape[1:], F32)
        kt[...] = ks[...].astype(F32).T.astype(BF16)

        def body(i, carry):
            place = pl.ds(pl.multiple_of(i * TILE, TILE), TILE)
            q = qs[place, :]
            g = gs[place, :]
            nt = (((1,), (1,)), ((), ()))
            s = lax.dot_general(ks[...], q, nt, preferred_element_type=F32)
            dp = lax.dot_general(vs[...], g, nt, preferred_element_type=F32)
            e = jnp.exp2((s - jnp.max(s, 0, keepdims=True)) * factor)
            inverse = 1.0 / jnp.sum(e, 0, keepdims=True)
            p = e * inverse
            dot = jnp.sum(p * dp, 0, keepdims=True)
            slopes = (p * (dp - dot)).astype(BF16)
            acc[t, 0] += jnp.dot(slopes, q, preferred_element_type=F32)
            acc[t, 1] += jnp.dot(p.astype(BF16), g, preferred_element_type=F32)
            dqs[place, :] = jnp.dot(kt[...], slopes, preferred_element_type=F32).T
            return carry

        lax.fori_loop(0, heads * queries // TILE, body, 0)

    scale = HEAD_DIM ** (-0.5)

    def finish(t):
        r, n = sizes[t]
        dst = part(t, osend_a, osend_c)
        mask = low_lanes(queries)
        if t < 2:
            x = jnp.where(mask, dqs[0:queries], dqs[queries : 2 * queries])
        else:
            x = pack_head(True, dqs[0 : queries // 2], dqs[queries // 2 : queries])
        dst[:, 0:r, :] = (scale * x).astype(BF16).reshape(CHIPS, r, LANES)
        acc_copy(t).wait_recv()
        for which in range(2):
            x = acc[t, which, 0:half_keys, :]
            if t == 2:
                x = pack_head(True, x[: half_keys // 2], x[half_keys // 2 :])
                x = x + sib_acc[t, which, 0 : half_keys // 2, :]
            else:
                x = x + sib_acc[t, which]
            if which == 0:
                x = scale * x
            x = x.reshape(CHIPS, r + n, LANES)
            dst[:, (1 + which) * r : (2 + which) * r, :] = x[:, :r].astype(BF16)
            if t < 2:
                half = images // 2
                for j in range(half):
                    tsend[t, which * half + j] = x[:, r + j * share : r + (j + 1) * share]
            else:
                tterm_c[grp, :, which * n : (which + 1) * n, :] = x[:, r:]
        for step in range(1, CHIPS):
            out_copy(t, step).start()
        for step in range(1, images):
            grp_copy(t, step).start()
        if t < 2:
            tterm_a[t, grp] = tsend[t, grp]
        part(t, orecv_a, orecv_c)[z] = dst[z]

    def finish_text(t):
        terms = part(t, tterm_a, tterm_c)
        for step in range(1, images):
            grp_copy(t, step).wait_recv()
        total = terms[0]
        for image in range(1, images):
            total = total + terms[image]
        dst = part(t, tz_a, tz_c)
        dst[...] = total.astype(BF16)
        for step in range(1, CHIPS):
            tz_copy(t, step).start()
        if t < 2:
            tshare[t, grp, z] = dst[z]
        else:
            tzr_c[z] = dst[z]

    def share_text(t):
        for step in range(1, CHIPS):
            tz_copy(t, step).wait_recv()
        for step in range(1, images):
            share_copy(t, step).start()

    def place_out(t):
        r, n = sizes[t]
        src = part(t, orecv_a, orecv_c)
        for step in range(1, CHIPS):
            out_copy(t, step).wait_recv()
        for which, dst in ((0, dq_out), (1, dk_out), (2, dv_out)):
            place(t, src, which * r, r, dst)

    def place_text(t):
        r, n = sizes[t]
        if t < 2:
            for step in range(1, images):
                share_copy(t, step).wait_recv()
            half = images // 2
            for which, dst in ((0, dtk_out), (1, dtv_out)):
                for chip in range(CHIPS):
                    cols = slice((2 * chip + t) * LANES, (2 * chip + t + 1) * LANES)
                    for j in range(half):
                        dst[j * share : (j + 1) * share, cols] = tshare[t, which * half + j, chip]
            return
        for step in range(1, CHIPS):
            tz_copy(t, step).wait_recv()
        for which, dst in ((0, dtk_out), (1, dtv_out)):
            place(t, tzr_c, which * n, n, dst)

    def place(t, src, at, r, dst):
        if t < 2:
            for chip in range(CHIPS):
                cols = slice((2 * chip + t) * LANES, (2 * chip + t + 1) * LANES)
                dst[:, cols] = src[chip, at : at + r, :]
        else:
            for pair in range(2):
                cols = slice((8 + pair) * LANES, (9 + pair) * LANES)
                low = src[2 * pair, at : at + r, :].astype(F32)
                high = src[2 * pair + 1, at : at + r, :].astype(F32)
                mask = low_lanes(r)
                dst[0:r, cols] = jnp.where(mask, low, swapped(high)).astype(BF16)
                dst[r : 2 * r, cols] = jnp.where(mask, swapped(low), high).astype(BF16)

    for t in range(3):
        r, n = sizes[t]
        for step in range(1, CHIPS):
            in_copy(t, step).wait_recv()
        if t < 2:
            for step in range(1, images):
                spread_copy(t, step).wait_recv()
            for j in range(images):
                place_at = 4 * rows + j * share
                recv_a[t, :, place_at : place_at + share, :] = tgot[t, j]
        sib_copy(t).start()
        load_queries(t)
        load_keys(t, part(t, recv_a, recv_c), 0, 2 * r)
        sib_copy(t).wait_recv()
        load_keys(t, part(t, sib_a, sib_c), half_keys, 0)
        compute(t)
        if t == 2:
            middle = half_keys + half_keys // 2
            for which in range(2):
                acc[t, which, half_keys:middle, :] = pack_head(
                    True, acc[t, which, half_keys:middle, :], acc[t, which, middle:, :]
                )
        acc_copy(t).start()
        if t > 0:
            finish_text(t - 1)
        finish(t)
    finish_text(2)
    share_text(0)
    share_text(1)
    place_out(0)
    place_text(0)
    place_out(1)
    place_text(1)
    place_out(2)
    place_text(2)
    for t in range(3):
        for step in range(1, CHIPS):
            in_copy(t, step).wait_send()
            if t < 2:
                text_copy(t, step).wait_send()
            out_copy(t, step).wait_send()
            tz_copy(t, step).wait_send()
        for step in range(1, images):
            grp_copy(t, step).wait_send()
            if t < 2:
                share_copy(t, step).wait_send()
                spread_copy(t, step).wait_send()
        sib_copy(t).wait_send()
        acc_copy(t).wait_send()


def write_out(*refs):
    sems = refs[10]
    copies = [pltpu.make_async_copy(refs[i], refs[5 + i], sems.at[i]) for i in range(5)]
    for copy in copies:
        copy.start()
    for copy in copies:
        copy.wait()


def exchange(queries, image_keys, image_values, out_grad, text_keys, text_values, reward_ranks):
    rows = queries.shape[0]
    text = text_keys.shape[0]
    images = reward_ranks.shape[0]
    width = 4 * rows + 2 * text
    keys = 2 * CHIPS * (rows + text)
    asked = CHIPS * rows
    like = lambda x: jax.ShapeDtypeStruct(x.shape, BF16)

    def pair_and_single(count, n, dtype):
        return [
            pltpu.VMEM((2, count, n, LANES), dtype),
            pltpu.VMEM((count, n // 2, LANES), dtype),
        ]

    def text_terms(n):
        return [
            pltpu.VMEM((2, images, CHIPS, n // images, LANES), F32),
            pltpu.VMEM((2, images, CHIPS, n // images, LANES), F32),
            pltpu.VMEM((images, CHIPS, n // 2, LANES), F32),
        ]

    dma = pltpu.SemaphoreType.DMA
    results = pl.pallas_call(
        fused,
        out_shape=[like(x) for x in (queries, image_keys, image_values, text_keys, text_values)],
        in_specs=[pl.BlockSpec(memory_space=pltpu.SMEM)]
        + [pl.BlockSpec(memory_space=pltpu.VMEM)] * 6,
        out_specs=[pl.BlockSpec(memory_space=pltpu.VMEM)] * 5,
        scratch_shapes=pair_and_single(CHIPS, width, BF16)
        + pair_and_single(CHIPS, width, BF16)
        + pair_and_single(CHIPS, 2 * rows + 2 * text, BF16)
        + [
            pltpu.VMEM((2 * asked, LANES), BF16),
            pltpu.VMEM((2 * asked, LANES), BF16),
            pltpu.VMEM((keys, LANES), BF16),
            pltpu.VMEM((keys, LANES), BF16),
            pltpu.VMEM((LANES, keys), BF16),
            pltpu.VMEM((2 * asked, LANES), F32),
            pltpu.VMEM((3, 2, keys, LANES), F32),
            pltpu.VMEM((3, 2, keys // 2, LANES), F32),
        ]
        + pair_and_single(CHIPS, 3 * rows, BF16)
        + pair_and_single(CHIPS, 3 * rows, BF16)
        + text_terms(2 * text)
        + [
            pltpu.VMEM((2, CHIPS, 2 * text // images, LANES), BF16),
            pltpu.VMEM((CHIPS, text, LANES), BF16),
            pltpu.VMEM((2, images, CHIPS, 2 * text // images, LANES), BF16),
            pltpu.VMEM((CHIPS, text, LANES), BF16),
            pltpu.VMEM((2, images, CHIPS, 2 * text // images, LANES), BF16),
            pltpu.VMEM((2, images, CHIPS, 2 * text // images, LANES), BF16),
        ]
        + [dma((3, CHIPS)), dma((3, CHIPS)), dma((3,)), dma((3,)), dma((3,)), dma((3,))]
        + [dma((3, CHIPS)), dma((3, CHIPS)), dma((3, images)), dma((3, images))]
        + [dma((3, CHIPS)), dma((3, CHIPS)), dma((2, images)), dma((2, images))]
        + [dma((2, CHIPS)), dma((2, CHIPS)), dma((2, images)), dma((2, images))],
        compiler_params=pltpu.CompilerParams(
            collective_id=0, has_side_effects=True, vmem_limit_bytes=56 * 1024 * 1024
        ),
    )(reward_ranks, queries, image_keys, image_values, out_grad, text_keys, text_values)
    return pl.pallas_call(
        write_out,
        out_shape=[like(x) for x in results],
        in_specs=[pl.BlockSpec(memory_space=pltpu.VMEM)] * 5,
        out_specs=[pl.BlockSpec(memory_space=pl.ANY)] * 5,
        scratch_shapes=[dma((5,))],
    )(*results)


def solution(mesh):
    in_specs = (
        P(("grp", "seq"), None),
        P(("grp", "seq"), None),
        P(("grp", "seq"), None),
        P(("grp", "seq"), None),
        P("seq", None),
        P("seq", None),
        P(),
    )
    out_specs = (
        P(("grp", "seq"), None),
        P(("grp", "seq"), None),
        P(("grp", "seq"), None),
        P("seq", None),
        P("seq", None),
    )
    body = exchange if mesh.shape["seq"] == 2 * CHIPS else local
    return jax.shard_map(body, mesh=mesh, in_specs=in_specs, out_specs=out_specs, check_vma=False)
```
